32 devices in a mesh: parts: 2 (over y), rows: 8 (over z, x), tp: 2 (over core).
Axes of the slice: x: 2, y: 2, z: 4, core: 2. Of those that a mesh axis runs over, the one named last changes fastest.
Arguments:
- tokens: bfloat16 [256, 8192], P(('parts', 'rows'), 'tp'), parts along dimension 0, may hold values from -6 to 6
- gate_weight: bfloat16 [8192, 28672], P('tp', 'rows'), may hold values from -0.0625 to 0.0625
- down_panels: bfloat16 [8, 64, 8192], P('rows', None, 'tp'), may hold values from -0.0625 to 0.0625
- up_panels: bfloat16 [8, 64, 8, 2, 1792], P('rows', None, None, 'tp'), may hold values from -0.75 to 0.75
- adapter_scales: float32 [8], P('rows'), may hold values from 0.25 to 2
- adapter_per_row: int32 [256, 1], P('parts'), parts along dimension 0, may hold values from 0 to 7; in each aligned block of 128 rows (0 to 127, 128 to 255, ...) at most 32 rows name the same one
- storage_index_map: int32 [8], replicated, may hold values from 0 to 7, each once
Outputs:
- gate_out: bfloat16 [256, 28672], P('parts', ('rows', 'tp')), parts along dimension 0
The draws below stay inside these ranges and needn't reach their ends.
There are 2 independent parts, one for each index of `parts`. The reference program is written for one: setup_inputs(seed, part) draws one part's arguments, and reference() takes and returns one part's arrays. A program takes and returns all parts, laid end to end along the dimension named above; an argument that names none is the same for every part. Nothing has to cross between parts.
Inputs may be any that keep to these rules, and one draw needn't show every extreme that they name: `adapter_per_row`: at most 32 rows name one adapter, and one adapter is named by exactly 32 rows; every adapter is named by some row. A permutation: adapter a's panels and scale stand at index storage_index_map[a] of down_panels, up_panels and adapter_scales.
All inputs are finite; a program needn't handle non-finite values.
Results may differ from the reference program's by a relative error of at most 0.0051.
Values may be sent and summed in bfloat16 or wider, within the bound.
No kernel may reach another device: no remote copies, remote signals or barrier semaphores. Data moves between devices by JAX's collectives and lax.ppermute only.
A program may use at most 128 MiB of HBM per device.

```python
import math
import jax
import jax.numpy as jnp
import numpy as np

MODEL_WIDTH = 8192
HIDDEN_WIDTH = 28672
ADAPTER_RANK = 64
ROWS = 128
ADAPTER_COUNT = 8
CAP = 32
BLOCK_WIDTH = 1792
N_ROWS = 8
N_TP = 2


def shard_levels(key, extent, shards, least, largest):
    def one(dim, parts):
        heights = jax.random.uniform(jax.random.fold_in(jax.random.fold_in(key, 6), dim), (parts,), jnp.float32, least / len(shards), largest / len(shards))
        return jnp.repeat(jnp.exp(heights), extent[dim] // parts).reshape((-1,) + (1,) * (len(extent) - dim - 1))

    level = one(*shards[0])
    for cut in shards[1:]:
        level = level * one(*cut)
    return level


def assign_block(key, own, number, rows, count, top, bound, skew):
    ranking = jax.random.permutation(key, count)
    packed, ordinary = portions_of(count, rows * top, bound, skew, True), portions_of(count, rows * top, bound, skew, False)
    places = jnp.arange(count)

    def named(sizes, turn):
        used = int((sizes > 0).sum())
        fixed = max(1, used // 4)
        shifted = fixed + (places - fixed + turn * (used - fixed)) % max(1, count - fixed)
        return jnp.zeros((count,), jnp.int32).at[ranking[jnp.where(places < fixed, places, shifted)]].set(jnp.asarray(sizes, jnp.int32))

    sizes = jnp.where(number % 4 == 0, named(packed, number // 4), named(ordinary, number - number // 4 - 1))
    mixed = jax.random.permutation(jax.random.fold_in(own, 3), count)
    donor, taker = mixed[0:count // 2 * 2:2], mixed[1:count // 2 * 2:2]
    margin = jnp.minimum(sizes[donor] - 1, bound - sizes[taker]) // 2
    margin = jnp.where((donor == ranking[0]) | (taker == ranking[0]) | (sizes[taker] == 0), 0, jnp.maximum(margin, 0))
    shifted = jax.random.randint(jax.random.fold_in(own, 4), (count // 2,), 0, 1 << 20) % (margin + 1)
    sizes = sizes.at[donor].add(-shifted).at[taker].add(shifted)
    items = jnp.searchsorted(jnp.cumsum(sizes), jnp.arange(rows * top), side="right").astype(jnp.int32)
    table = items.reshape(top, rows).T
    table = table[jax.random.permutation(jax.random.fold_in(own, 1), rows)]
    turn = jax.random.randint(jax.random.fold_in(own, 2), (rows, 1), 0, top)
    return jnp.take_along_axis(table, (jnp.arange(top)[None, :] + turn) % top, axis=1)


def portions_of(count, total, most, lean, full):
    loads = [(1 << 20) // math.isqrt(grade ** lean) + 1 for grade in range(1, count + 1)]
    largest = most if full else min(most, max(-(-total // count), total * loads[0] // sum(loads)))
    least = 1 if total - largest >= count - 1 else 0
    holding, surplus = [largest] + [least] * (count - 1), total - largest - least * (count - 1)
    while surplus > 0:
        movable = [i for i in range(1, count) if holding[i] < largest] or [i for i in range(1, count) if holding[i] < most]
        pool, budget = sum([loads[i] for i in movable]), surplus
        for i in movable:
            extra = min(most - holding[i], max(1, budget * loads[i] // pool), surplus)
            holding[i] = holding[i] + extra
            surplus = surplus - extra
    return np.array(holding)


def gaussian(stream_key, extent, deviation, limit, split=(), kind=jnp.bfloat16):
    values = deviation * jax.random.normal(stream_key, extent, jnp.float32)
    if split:
        values = values * shard_levels(stream_key, extent, split, -0.22, 0.18)
    return jnp.clip(values, -limit, limit).astype(kind)


def setup_inputs(seed: int = 0, part: int = 0) -> dict:
    key_of = jax.random.split(jax.random.key(seed), 8)
    part_splits = jax.random.split(jax.random.fold_in(key_of[7], part), 8)
    tokens = gaussian(part_splits[0], (ROWS, MODEL_WIDTH), 1.0, 6.0, ((0, 8), (1, 2)))
    gate_weight = gaussian(key_of[1], (MODEL_WIDTH, HIDDEN_WIDTH), MODEL_WIDTH ** -0.5, 0.0625, ((0, 2), (1, 8)))
    down_panels = gaussian(key_of[2], (ADAPTER_COUNT, ADAPTER_RANK, MODEL_WIDTH), MODEL_WIDTH ** -0.5, 0.0625, ((0, 8), (2, 2)))
    up_panels = gaussian(key_of[3], (ADAPTER_COUNT, ADAPTER_RANK, N_ROWS, N_TP, BLOCK_WIDTH), ADAPTER_RANK ** -0.5, 0.75, ((0, 8), (3, 2)))
    adapter_scales = jnp.clip(jnp.exp(math.log(2.0) - 2.0794415 * jax.random.uniform(key_of[4], (ADAPTER_COUNT,), jnp.float32) ** shard_levels(key_of[4], (ADAPTER_COUNT,), ((0, 8),), -0.2, 0.2)), 0.25, 2.0)
    adapter_per_row_keys = jax.random.split(jax.random.fold_in(part_splits[5], 1), ROWS // ROWS)
    adapter_per_row_turns = jax.random.permutation(jax.random.fold_in(part_splits[5], 3), ROWS // ROWS)
    adapter_per_row = jax.vmap(lambda own, number: assign_block(jax.random.fold_in(part_splits[5], 2), own, number, ROWS, ADAPTER_COUNT, 1, CAP, 2))(adapter_per_row_keys, adapter_per_row_turns).reshape((ROWS, 1))
    storage_index_map = jax.random.permutation(key_of[6], ADAPTER_COUNT).astype(jnp.int32)
    return dict(tokens=tokens, gate_weight=gate_weight, down_panels=down_panels, up_panels=up_panels, adapter_scales=adapter_scales, adapter_per_row=adapter_per_row, storage_index_map=storage_index_map)


def slot_layout(adapter_per_row, storage_index_map, owner_indices, slot_depth):
    row_total = adapter_per_row.shape[0]
    stored = jnp.take(storage_index_map, adapter_per_row[:, 0], axis=0).astype(jnp.int32)
    row_order = jnp.argsort(stored, stable=True).astype(jnp.int32)
    arranged = jnp.take(stored, row_order, axis=0)
    matches = (stored[:, None] == jnp.arange(owner_indices, dtype=jnp.int32)[None, :]).astype(jnp.int32)
    counts = jnp.sum(matches, axis=0)
    starts = jnp.cumsum(counts) - counts
    within = jnp.arange(row_total, dtype=jnp.int32) - jnp.take(starts, arranged, axis=0)
    placed = (arranged * slot_depth + within).astype(jnp.int32)
    slot_of_row = jnp.zeros((row_total,), jnp.int32).at[row_order].set(placed)
    row_of_slot = jnp.full((owner_indices * slot_depth,), row_total, jnp.int32).at[slot_of_row].set(jnp.arange(row_total, dtype=jnp.int32))
    return slot_of_row, row_of_slot


def reference(tokens, gate_weight, down_panels, up_panels, adapter_scales, adapter_per_row, storage_index_map):
    owner_indices = down_panels.shape[0]
    slot_of_row, row_of_slot = slot_layout(adapter_per_row, storage_index_map, owner_indices, CAP)
    base = jnp.dot(tokens, gate_weight, preferred_element_type=jnp.float32)
    padded = jnp.concatenate([tokens, jnp.zeros((1, MODEL_WIDTH), tokens.dtype)], axis=0)
    selected_panels = jnp.take(padded, row_of_slot, axis=0).reshape(owner_indices, CAP, MODEL_WIDTH)
    reduced_rank = jnp.einsum("lme,lje->lmj", selected_panels.astype(jnp.float32), down_panels.astype(jnp.float32))
    reduced_rank = adapter_scales[:, None, None] * reduced_rank
    lowrank_b = reduced_rank.astype(jnp.bfloat16)
    panel_stack = up_panels.reshape(owner_indices, ADAPTER_RANK, HIDDEN_WIDTH)
    delta = jnp.einsum("ocr,orf->ocf", lowrank_b.astype(jnp.float32), panel_stack.astype(jnp.float32)).astype(jnp.bfloat16)
    delta_rows = jnp.take(delta.reshape(owner_indices * CAP, HIDDEN_WIDTH), slot_of_row, axis=0)
    return (base + delta_rows.astype(jnp.float32)).astype(jnp.bfloat16)
```

```python
import functools

import jax
import jax.numpy as jnp
from jax import lax
from jax.experimental import pallas as pl
from jax.experimental.pallas import tpu as pltpu
from jax.sharding import PartitionSpec as P

CAP = 32
F32 = jnp.float32
BF16 = jnp.bfloat16
VMEM = pl.BlockSpec(memory_space=pltpu.VMEM)
SMEM = pl.BlockSpec(memory_space=pltpu.SMEM)


def slot_layout(adapter_per_row, storage_index_map, owner_indices, slot_depth):
    row_total = adapter_per_row.shape[0]
    stored = jnp.take(storage_index_map, adapter_per_row[:, 0], axis=0)
    row_order = jnp.argsort(stored, stable=True)
    arranged = jnp.take(stored, row_order, axis=0)
    matches = (stored[:, None] == jnp.arange(owner_indices, dtype=jnp.int32)[None, :]).astype(
        jnp.int32
    )
    counts = jnp.sum(matches, axis=0)
    starts = jnp.cumsum(counts) - counts
    within = jnp.arange(row_total, dtype=jnp.int32) - jnp.take(starts, arranged, axis=0)
    placed = arranged * slot_depth + within
    slot_of_row = jnp.zeros((row_total,), jnp.int32).at[row_order].set(placed)
    row_of_slot = (
        jnp.full((owner_indices * slot_depth,), row_total, jnp.int32)
        .at[slot_of_row]
        .set(jnp.arange(row_total, dtype=jnp.int32))
    )
    return (slot_of_row, row_of_slot)


def many_groups(
    tokens, gate_weight, down_panels, up_panels, adapter_scales, adapter_per_row, storage_index_map
):
    owner_indices = lax.axis_size("rows")
    myself = lax.axis_index("rows")
    slot_of_row, row_of_slot = slot_layout(adapter_per_row, storage_index_map, owner_indices, CAP)
    my_rows = lax.dynamic_slice_in_dim(row_of_slot, myself * CAP, CAP, 0)
    piece = lax.all_gather(tokens, "rows", axis=0, tiled=True)
    inside = my_rows < piece.shape[0]
    taken = jnp.take(piece, jnp.clip(my_rows, 0, piece.shape[0] - 1), axis=0)
    selected = jnp.where(inside[:, None], taken, jnp.zeros_like(taken))
    block = jnp.dot(piece, gate_weight, preferred_element_type=F32)
    halves = lax.psum_scatter(block, "tp", scatter_dimension=1, tiled=True)
    width = up_panels.shape[-1]
    low = lax.dot_general(
        selected, down_panels[0], (((1,), (1,)), ((), ())), preferred_element_type=F32
    )
    low = low + lax.ppermute(low, "tp", [(0, 1), (1, 0)])
    low = (low * adapter_scales[0]).astype(BF16)
    panel = up_panels.reshape(down_panels.shape[1], owner_indices, width)
    delta = jnp.einsum("cr,rof->ocf", low, panel, preferred_element_type=F32).astype(BF16)
    arrived = lax.all_to_all(delta, "rows", split_axis=0, concat_axis=0, tiled=True)
    delta_rows = jnp.take(arrived.reshape(owner_indices * CAP, width), slot_of_row, axis=0)
    return (halves + delta_rows.astype(F32)).astype(BF16)


def slots_as_row(adapter_ref, map_ref):
    rows = adapter_ref.shape[1]
    count = map_ref.shape[0]
    adapter = adapter_ref[...]
    stored = jnp.zeros_like(adapter)
    for a in range(count):
        stored = jnp.where(adapter == a, map_ref[a], stored)
    index = lax.broadcasted_iota(jnp.int32, (count, rows), 0)
    match = (stored == index).astype(F32)
    earlier = (
        lax.broadcasted_iota(jnp.int32, (rows, rows), 0)
        < lax.broadcasted_iota(jnp.int32, (rows, rows), 1)
    ).astype(F32)
    before = jnp.dot(match.astype(BF16), earlier.astype(BF16), preferred_element_type=F32)
    within = jnp.sum(match * before, axis=0, keepdims=True)
    return stored * CAP + within.astype(jnp.int32)


def lowrank_kernel(groups, *refs):
    where, index_map, adapter = refs[:3]
    pieces = refs[3 : 3 + groups]
    down, out, gathered = refs[3 + groups :]
    me = where[0]
    part = pieces[0].shape[0]
    for d in range(groups):
        start = pl.multiple_of((me ^ d) * part, part)
        gathered[pl.ds(start, part), :] = pieces[d][...]
    slot = slots_as_row(adapter, index_map)
    rows = slot.shape[1]
    mine = lax.broadcasted_iota(jnp.int32, (CAP, rows), 0) + me * CAP
    chosen = (slot == mine).astype(F32).astype(BF16)
    selected = jnp.dot(chosen, gathered[...], preferred_element_type=F32).astype(BF16)
    out[...] = lax.dot_general(
        selected, down[...], (((1,), (1,)), ((), ())), preferred_element_type=F32
    )


def delta_kernel(groups, scale, low_a, low_b, up, out, spread):
    rank = low_a.shape[1]
    low = ((low_a[...] + low_b[...]) * scale[0]).astype(BF16)
    depth = rank * groups
    widen = (
        lax.broadcasted_iota(jnp.int32, (rank, depth), 0)
        == lax.broadcasted_iota(jnp.int32, (rank, depth), 1) // groups
    ).astype(F32).astype(BF16)
    wide = jnp.dot(low, widen, preferred_element_type=F32)
    block = lax.rem(lax.broadcasted_iota(jnp.int32, (CAP, depth), 1), groups)
    for d in range(groups):
        spread[d * CAP : (d + 1) * CAP, :] = jnp.where(block == d, wide, 0.0).astype(BF16)
    result = jnp.dot(spread[...], up[...], preferred_element_type=F32)
    out[...] = result.astype(BF16)


def base_kernel(groups, *refs):
    where = refs[0]
    pieces = refs[1 : 1 + groups]
    weight, _, out, gathered = refs[1 + groups :]
    me = where[0]
    part = pieces[0].shape[0]

    @pl.when(pl.program_id(0) == 0)
    def _():
        for d in range(groups):
            start = pl.multiple_of((me ^ d) * part, part)
            gathered[pl.ds(start, part), :] = pieces[d][...]

    out[...] = jnp.dot(gathered[...], weight[...], preferred_element_type=F32)


def final_kernel(groups, index_map, adapter, own, other, arrived, out):
    slot = slots_as_row(adapter, index_map)
    rows = slot.shape[1]
    place = (
        slot == lax.broadcasted_iota(jnp.int32, (groups * CAP, rows), 0)
    ).astype(F32).astype(BF16)
    delta = lax.dot_general(
        place, arrived[...], (((0,), (0,)), ((), ())), preferred_element_type=F32
    )
    out[...] = (own[...] + other[...] + delta).astype(BF16)


def few_groups(
    tokens, gate_weight, down_panels, up_panels, adapter_scales, adapter_per_row, storage_index_map
):
    groups = lax.axis_size("rows")
    me = lax.axis_index("rows").astype(jnp.int32)
    core = lax.axis_index("tp").astype(jnp.int32)
    part, depth = tokens.shape
    rows = part * groups
    rank = down_panels.shape[1]
    width = up_panels.shape[-1]
    where = me.reshape(1)
    adapter = adapter_per_row.reshape(1, rows)
    swap = [(0, 1), (1, 0)]

    def to(x, d):
        return lax.ppermute(x, "rows", [(i, i ^ d) for i in range(groups)])

    pieces = {0: tokens}
    for d in range(2, groups, 2):
        pieces[d] = to(tokens, d)
    if groups > 1:
        for d in range(0, groups, 2):
            pieces[d + 1] = to(pieces[d], 1)
    pieces = [pieces[d] for d in range(groups)]

    low = pl.pallas_call(
        functools.partial(lowrank_kernel, groups),
        out_shape=jax.ShapeDtypeStruct((CAP, rank), F32),
        in_specs=[SMEM, SMEM, VMEM] + [VMEM] * groups + [VMEM],
        out_specs=VMEM,
        scratch_shapes=[pltpu.VMEM((rows, depth), BF16)],
        compiler_params=pltpu.CompilerParams(vmem_limit_bytes=16 << 20),
        cost_estimate=pl.CostEstimate(flops=10**8, bytes_accessed=2 * 10**6, transcendentals=0),
        name="lowrank",
    )(where, storage_index_map, adapter, *pieces, down_panels[0])
    low_other = lax.ppermute(low, "tp", swap)

    deltas = pl.pallas_call(
        functools.partial(delta_kernel, groups),
        out_shape=jax.ShapeDtypeStruct((groups * CAP, width), BF16),
        in_specs=[SMEM, VMEM, VMEM, VMEM],
        out_specs=VMEM,
        scratch_shapes=[pltpu.VMEM((groups * CAP, rank * groups), BF16)],
        compiler_params=pltpu.CompilerParams(vmem_limit_bytes=32 << 20),
        cost_estimate=pl.CostEstimate(flops=5 * 10**8, bytes_accessed=3 * 10**6, transcendentals=0),
        name="delta",
    )(adapter_scales, low, low_other, up_panels.reshape(rank * groups, width))
    arrived = lax.all_to_all(deltas, "rows", split_axis=0, concat_axis=0, tiled=True)

    tile = 256

    def base(which, after):
        steps = width // tile
        return pl.pallas_call(
            functools.partial(base_kernel, groups),
            grid_spec=pltpu.PrefetchScalarGridSpec(
                num_scalar_prefetch=1,
                grid=(steps,),
                in_specs=[pl.BlockSpec((part, depth), lambda i, s: (0, 0))] * groups
                + [pl.BlockSpec((depth, tile), lambda i, s: (0, s[1] * steps + i))]
                + [pl.BlockSpec(memory_space=pl.ANY)],
                out_specs=pl.BlockSpec((rows, tile), lambda i, s: (0, i)),
                scratch_shapes=[pltpu.VMEM((rows, depth), BF16)],
            ),
            out_shape=jax.ShapeDtypeStruct((rows, width), F32),
            compiler_params=pltpu.CompilerParams(vmem_limit_bytes=32 << 20),
            cost_estimate=pl.CostEstimate(
                flops=rows * depth,
                bytes_accessed=2 * depth,
                transcendentals=0,
            ),
            name="base",
        )(jnp.stack([me, which]), *pieces, gate_weight, after)

    partner = base(1 - core, deltas)
    other = lax.ppermute(partner, "tp", swap)
    own = base(core, partner)

    return pl.pallas_call(
        functools.partial(final_kernel, groups),
        out_shape=jax.ShapeDtypeStruct((rows, width), BF16),
        in_specs=[SMEM, VMEM, VMEM, VMEM, VMEM],
        out_specs=VMEM,
        compiler_params=pltpu.CompilerParams(vmem_limit_bytes=32 << 20),
        cost_estimate=pl.CostEstimate(flops=2 * 10**8, bytes_accessed=4 * 10**6, transcendentals=0),
        name="combine",
    )(storage_index_map, adapter, own, other, arrived)


def on_device(*args):
    if lax.axis_size("rows") in (2, 4, 8):
        return few_groups(*args)
    return many_groups(*args)


def solution(mesh):
    placed = (
        P(("parts", "rows"), "tp"),
        P("tp", "rows"),
        P("rows", None, "tp"),
        P("rows", None, None, "tp", None),
        P("rows"),
        P("parts", None),
        P(),
    )
    return jax.shard_map(
        on_device, mesh=mesh, in_specs=placed, out_specs=P("parts", ("rows", "tp")), check_vma=False
    )
```

```python
import functools

import jax
import jax.numpy as jnp
from jax import lax
from jax.experimental import pallas as pl
from jax.experimental.pallas import tpu as pltpu
from jax.sharding import PartitionSpec as P

CAP = 32
F32 = jnp.float32
BF16 = jnp.bfloat16
VMEM = pl.BlockSpec(memory_space=pltpu.VMEM)
SMEM = pl.BlockSpec(memory_space=pltpu.SMEM)
ANY = pl.BlockSpec(memory_space=pl.ANY)


def slot_layout(adapter_per_row, storage_index_map, owner_indices, slot_depth):
    row_total = adapter_per_row.shape[0]
    stored = jnp.take(storage_index_map, adapter_per_row[:, 0], axis=0)
    row_order = jnp.argsort(stored, stable=True)
    arranged = jnp.take(stored, row_order, axis=0)
    matches = (stored[:, None] == jnp.arange(owner_indices, dtype=jnp.int32)[None, :]).astype(
        jnp.int32
    )
    counts = jnp.sum(matches, axis=0)
    starts = jnp.cumsum(counts) - counts
    within = jnp.arange(row_total, dtype=jnp.int32) - jnp.take(starts, arranged, axis=0)
    placed = arranged * slot_depth + within
    slot_of_row = jnp.zeros((row_total,), jnp.int32).at[row_order].set(placed)
    row_of_slot = (
        jnp.full((owner_indices * slot_depth,), row_total, jnp.int32)
        .at[slot_of_row]
        .set(jnp.arange(row_total, dtype=jnp.int32))
    )
    return (slot_of_row, row_of_slot)


def many_groups(
    tokens, gate_weight, down_panels, up_panels, adapter_scales, adapter_per_row, storage_index_map
):
    owner_indices = lax.axis_size("rows")
    myself = lax.axis_index("rows")
    slot_of_row, row_of_slot = slot_layout(adapter_per_row, storage_index_map, owner_indices, CAP)
    my_rows = lax.dynamic_slice_in_dim(row_of_slot, myself * CAP, CAP, 0)
    piece = lax.all_gather(tokens, "rows", axis=0, tiled=True)
    inside = my_rows < piece.shape[0]
    taken = jnp.take(piece, jnp.clip(my_rows, 0, piece.shape[0] - 1), axis=0)
    selected = jnp.where(inside[:, None], taken, jnp.zeros_like(taken))
    block = jnp.dot(piece, gate_weight, preferred_element_type=F32)
    halves = lax.psum_scatter(block, "tp", scatter_dimension=1, tiled=True)
    width = up_panels.shape[-1]
    low = lax.dot_general(
        selected, down_panels[0], (((1,), (1,)), ((), ())), preferred_element_type=F32
    )
    low = low + lax.ppermute(low, "tp", [(0, 1), (1, 0)])
    low = (low * adapter_scales[0]).astype(BF16)
    panel = up_panels.reshape(down_panels.shape[1], owner_indices, width)
    delta = jnp.einsum("cr,rof->ocf", low, panel, preferred_element_type=F32).astype(BF16)
    arrived = lax.all_to_all(delta, "rows", split_axis=0, concat_axis=0, tiled=True)
    delta_rows = jnp.take(arrived.reshape(owner_indices * CAP, width), slot_of_row, axis=0)
    return (halves + delta_rows.astype(F32)).astype(BF16)


def slots_as_row(adapter_ref, map_ref):
    rows = adapter_ref.shape[1]
    count = map_ref.shape[0]
    adapter = adapter_ref[...]
    stored = jnp.zeros_like(adapter)
    for a in range(count):
        stored = jnp.where(adapter == a, map_ref[a], stored)
    index = lax.broadcasted_iota(jnp.int32, (count, rows), 0)
    match = (stored == index).astype(F32)
    earlier = (
        lax.broadcasted_iota(jnp.int32, (rows, rows), 0)
        < lax.broadcasted_iota(jnp.int32, (rows, rows), 1)
    ).astype(F32)
    before = jnp.dot(match.astype(BF16), earlier.astype(BF16), preferred_element_type=F32)
    within = jnp.sum(match * before, axis=0, keepdims=True)
    return stored * CAP + within.astype(jnp.int32)


def first_kernel(
    index_map, adapter, tokens, down, up, slot, tokens_here, down_here, up_here, arrival
):
    copies = [
        pltpu.make_async_copy(tokens, tokens_here, arrival.at[0]),
        pltpu.make_async_copy(down, down_here, arrival.at[1]),
        pltpu.make_async_copy(up, up_here, arrival.at[2]),
    ]
    for copy in copies:
        copy.start()
    slot[...] = slots_as_row(adapter, index_map)
    for copy in copies:
        copy.wait()


def lowrank_kernel(groups, *refs):
    where, slots = refs[:2]
    pieces = refs[2 : 2 + groups]
    down, out, gathered = refs[2 + groups :]
    me = where[0]
    part = pieces[0].shape[0]
    for d in range(groups):
        start = pl.multiple_of((me ^ d) * part, part)
        gathered[pl.ds(start, part), :] = pieces[d][...]
    slot = slots[...]
    rows = slot.shape[1]
    mine = lax.broadcasted_iota(jnp.int32, (CAP, rows), 0) + me * CAP
    chosen = (slot == mine).astype(F32).astype(BF16)
    selected = jnp.dot(chosen, gathered[...], preferred_element_type=F32).astype(BF16)
    out[...] = lax.dot_general(
        selected, down[...], (((1,), (1,)), ((), ())), preferred_element_type=F32
    )


def delta_kernel(groups, scale, low_a, low_b, up, out, spread):
    rank = low_a.shape[1]
    low = ((low_a[...] + low_b[...]) * scale[0]).astype(BF16)
    depth = rank * groups
    widen = (
        lax.broadcasted_iota(jnp.int32, (rank, depth), 0)
        == lax.broadcasted_iota(jnp.int32, (rank, depth), 1) // groups
    ).astype(F32).astype(BF16)
    wide = jnp.dot(low, widen, preferred_element_type=F32)
    block = lax.rem(lax.broadcasted_iota(jnp.int32, (CAP, depth), 1), groups)
    for d in range(groups):
        spread[d * CAP : (d + 1) * CAP, :] = jnp.where(block == d, wide, 0.0).astype(BF16)
    result = jnp.dot(spread[...], up[...], preferred_element_type=F32)
    out[...] = result.astype(BF16)


def base_kernel(groups, tile, slots, *refs):
    where = refs[0]
    pieces = refs[1 : 1 + groups]
    weight, _, partner, own, gathered, held, arrival = refs[1 + groups :]
    me, core = where[0], where[1]
    part = pieces[0].shape[0]
    width = own.shape[1]
    count = width // tile

    def fetch(step):
        half = 1 - core if step < count else core
        start = half * width + (step % count) * tile
        return pltpu.make_async_copy(
            weight.at[:, pl.ds(pl.multiple_of(start, 128), tile)],
            held.at[step % slots],
            arrival.at[step % slots],
        )

    for step in range(slots - 1):
        fetch(step).start()
    for d in range(groups):
        start = pl.multiple_of((me ^ d) * part, part)
        gathered[pl.ds(start, part), :] = pieces[d][...]
    for step in range(2 * count):
        if step + slots - 1 < 2 * count:
            fetch(step + slots - 1).start()
        fetch(step).wait()
        out = partner if step < count else own
        start = (step % count) * tile
        out[:, start : start + tile] = jnp.dot(
            gathered[...], held[step % slots], preferred_element_type=F32
        )


def final_kernel(groups, slots, own, other, arrived, out):
    slot = slots[...]
    rows = slot.shape[1]
    place = (
        slot == lax.broadcasted_iota(jnp.int32, (groups * CAP, rows), 0)
    ).astype(F32).astype(BF16)
    delta = lax.dot_general(
        place, arrived[...], (((0,), (0,)), ((), ())), preferred_element_type=F32
    )
    out[...] = (own[...] + other[...] + delta).astype(BF16)


def few_groups(
    tokens, gate_weight, down_panels, up_panels, adapter_scales, adapter_per_row, storage_index_map
):
    groups = lax.axis_size("rows")
    me = lax.axis_index("rows").astype(jnp.int32)
    core = lax.axis_index("tp").astype(jnp.int32)
    part, depth = tokens.shape
    rows = part * groups
    rank = down_panels.shape[1]
    width = up_panels.shape[-1]
    where = me.reshape(1)
    adapter = adapter_per_row.reshape(1, rows)
    swap = [(0, 1), (1, 0)]

    def to(x, d):
        return lax.ppermute(x, "rows", [(i, i ^ d) for i in range(groups)])

    def params(limit):
        return pltpu.CompilerParams(vmem_limit_bytes=limit << 20)

    slot, tokens_here, down_here, up_here = pl.pallas_call(
        first_kernel,
        out_shape=[
            jax.ShapeDtypeStruct((1, rows), jnp.int32),
            jax.ShapeDtypeStruct((part, depth), BF16),
            jax.ShapeDtypeStruct((rank, depth), BF16),
            jax.ShapeDtypeStruct((rank * groups, width), BF16),
        ],
        in_specs=[SMEM, VMEM] + [ANY] * 3,
        out_specs=[VMEM] * 4,
        scratch_shapes=[pltpu.SemaphoreType.DMA((3,))],
        compiler_params=params(48),
        cost_estimate=pl.CostEstimate(flops=10**6, bytes_accessed=5 * 10**6, transcendentals=0),
        name="first",
    )(storage_index_map, adapter, tokens, down_panels[0], up_panels.reshape(rank * groups, width))

    pieces = {0: tokens_here}
    for d in range(2, groups, 2):
        pieces[d] = to(tokens, d)
    for d in range(0, groups, 2):
        pieces[d + 1] = to(pieces[d], 1)
    pieces = [pieces[d] for d in range(groups)]

    low = pl.pallas_call(
        functools.partial(lowrank_kernel, groups),
        out_shape=jax.ShapeDtypeStruct((CAP, rank), F32),
        in_specs=[SMEM, VMEM] + [VMEM] * groups + [VMEM],
        out_specs=VMEM,
        scratch_shapes=[pltpu.VMEM((rows, depth), BF16)],
        compiler_params=params(8),
        cost_estimate=pl.CostEstimate(flops=10**8, bytes_accessed=2 * 10**6, transcendentals=0),
        name="lowrank",
    )(where, slot, *pieces, down_here)
    low_other = lax.ppermute(low, "tp", swap)

    deltas = pl.pallas_call(
        functools.partial(delta_kernel, groups),
        out_shape=jax.ShapeDtypeStruct((groups * CAP, width), BF16),
        in_specs=[SMEM, VMEM, VMEM, VMEM],
        out_specs=VMEM,
        scratch_shapes=[pltpu.VMEM((groups * CAP, rank * groups), BF16)],
        compiler_params=params(8),
        cost_estimate=pl.CostEstimate(flops=5 * 10**8, bytes_accessed=3 * 10**6, transcendentals=0),
        name="delta",
    )(adapter_scales, low, low_other, up_here)
    arrived = lax.all_to_all(deltas, "rows", split_axis=0, concat_axis=0, tiled=True)

    tile, buffers = 256, 5
    half = jax.ShapeDtypeStruct((rows, width), F32)
    partner, own = pl.pallas_call(
        functools.partial(base_kernel, groups, tile, buffers),
        in_specs=[SMEM] + [VMEM] * groups + [ANY, ANY],
        out_specs=[VMEM, VMEM],
        scratch_shapes=[
            pltpu.VMEM((rows, depth), BF16),
            pltpu.VMEM((buffers, depth, tile), BF16),
            pltpu.SemaphoreType.DMA((buffers,)),
        ],
        out_shape=[half, half],
        compiler_params=params(40),
        cost_estimate=pl.CostEstimate(
            flops=4 * rows * depth * width, bytes_accessed=10**7, transcendentals=0
        ),
        name="base",
    )(jnp.stack([me, core]), *pieces, gate_weight, deltas)
    other = lax.ppermute(partner, "tp", swap)

    return pl.pallas_call(
        functools.partial(final_kernel, groups),
        out_shape=jax.ShapeDtypeStruct((rows, width), BF16),
        in_specs=[VMEM, VMEM, VMEM, VMEM],
        out_specs=VMEM,
        compiler_params=params(8),
        cost_estimate=pl.CostEstimate(flops=2 * 10**8, bytes_accessed=4 * 10**6, transcendentals=0),
        name="combine",
    )(slot, own, other, arrived)


def on_device(*args):
    if lax.axis_size("rows") in (2, 4, 8):
        return few_groups(*args)
    return many_groups(*args)


def solution(mesh):
    placed = (
        P(("parts", "rows"), "tp"),
        P("tp", "rows"),
        P("rows", None, "tp"),
        P("rows", None, None, "tp", None),
        P("rows"),
        P("parts", None),
        P(),
    )
    return jax.shard_map(
        on_device, mesh=mesh, in_specs=placed, out_specs=P("parts", ("rows", "tp")), check_vma=False
    )
```

```python
import functools

import jax
import jax.numpy as jnp
from jax import lax
from jax.experimental import pallas as pl
from jax.experimental.pallas import tpu as pltpu
from jax.sharding import PartitionSpec as P

CAP = 32
F32 = jnp.float32
BF16 = jnp.bfloat16
VMEM = pl.BlockSpec(memory_space=pltpu.VMEM)
SMEM = pl.BlockSpec(memory_space=pltpu.SMEM)
ANY = pl.BlockSpec(memory_space=pl.ANY)


def slot_layout(adapter_per_row, storage_index_map, owner_indices, slot_depth):
    row_total = adapter_per_row.shape[0]
    stored = jnp.take(storage_index_map, adapter_per_row[:, 0], axis=0)
    row_order = jnp.argsort(stored, stable=True)
    arranged = jnp.take(stored, row_order, axis=0)
    matches = (stored[:, None] == jnp.arange(owner_indices, dtype=jnp.int32)[None, :]).astype(
        jnp.int32
    )
    counts = jnp.sum(matches, axis=0)
    starts = jnp.cumsum(counts) - counts
    within = jnp.arange(row_total, dtype=jnp.int32) - jnp.take(starts, arranged, axis=0)
    placed = arranged * slot_depth + within
    slot_of_row = jnp.zeros((row_total,), jnp.int32).at[row_order].set(placed)
    row_of_slot = (
        jnp.full((owner_indices * slot_depth,), row_total, jnp.int32)
        .at[slot_of_row]
        .set(jnp.arange(row_total, dtype=jnp.int32))
    )
    return (slot_of_row, row_of_slot)


def many_groups(
    tokens, gate_weight, down_panels, up_panels, adapter_scales, adapter_per_row, storage_index_map
):
    owner_indices = lax.axis_size("rows")
    myself = lax.axis_index("rows")
    slot_of_row, row_of_slot = slot_layout(adapter_per_row, storage_index_map, owner_indices, CAP)
    my_rows = lax.dynamic_slice_in_dim(row_of_slot, myself * CAP, CAP, 0)
    piece = lax.all_gather(tokens, "rows", axis=0, tiled=True)
    inside = my_rows < piece.shape[0]
    taken = jnp.take(piece, jnp.clip(my_rows, 0, piece.shape[0] - 1), axis=0)
    selected = jnp.where(inside[:, None], taken, jnp.zeros_like(taken))
    block = jnp.dot(piece, gate_weight, preferred_element_type=F32)
    halves = lax.psum_scatter(block, "tp", scatter_dimension=1, tiled=True)
    width = up_panels.shape[-1]
    low = lax.dot_general(
        selected, down_panels[0], (((1,), (1,)), ((), ())), preferred_element_type=F32
    )
    low = low + lax.ppermute(low, "tp", [(0, 1), (1, 0)])
    low = (low * adapter_scales[0]).astype(BF16)
    panel = up_panels.reshape(down_panels.shape[1], owner_indices, width)
    delta = jnp.einsum("cr,rof->ocf", low, panel, preferred_element_type=F32).astype(BF16)
    arrived = lax.all_to_all(delta, "rows", split_axis=0, concat_axis=0, tiled=True)
    delta_rows = jnp.take(arrived.reshape(owner_indices * CAP, width), slot_of_row, axis=0)
    return (halves + delta_rows.astype(F32)).astype(BF16)


def slots_as_row(adapter_ref, map_ref):
    rows = adapter_ref.shape[1]
    count = map_ref.shape[0]
    adapter = adapter_ref[...]
    stored = jnp.zeros_like(adapter)
    for a in range(count):
        stored = jnp.where(adapter == a, map_ref[a], stored)
    index = lax.broadcasted_iota(jnp.int32, (count, rows), 0)
    match = (stored == index).astype(F32)
    earlier = (
        lax.broadcasted_iota(jnp.int32, (rows, rows), 0)
        < lax.broadcasted_iota(jnp.int32, (rows, rows), 1)
    ).astype(F32)
    before = jnp.dot(match.astype(BF16), earlier.astype(BF16), preferred_element_type=F32)
    within = jnp.sum(match * before, axis=0, keepdims=True)
    return stored * CAP + within.astype(jnp.int32)


def slots_kernel(index_map, adapter, slot):
    slot[...] = slots_as_row(adapter, index_map)


def lowrank_kernel(groups, *refs):
    where, slots = refs[:2]
    pieces = refs[2 : 2 + groups]
    down, out, gathered = refs[2 + groups :]
    me = where[0]
    part = pieces[0].shape[0]
    for d in range(groups):
        start = pl.multiple_of((me ^ d) * part, part)
        gathered[pl.ds(start, part), :] = pieces[d][...]
    slot = slots[...]
    rows = slot.shape[1]
    mine = lax.broadcasted_iota(jnp.int32, (CAP, rows), 0) + me * CAP
    chosen = (slot == mine).astype(F32).astype(BF16)
    selected = jnp.dot(chosen, gathered[...], preferred_element_type=F32).astype(BF16)
    out[...] = lax.dot_general(
        selected, down[...], (((1,), (1,)), ((), ())), preferred_element_type=F32
    )


def delta_kernel(groups, scale, low_a, low_b, up, out, spread):
    rank = low_a.shape[1]
    low = ((low_a[...] + low_b[...]) * scale[0]).astype(BF16)
    depth = rank * groups
    widen = (
        lax.broadcasted_iota(jnp.int32, (rank, depth), 0)
        == lax.broadcasted_iota(jnp.int32, (rank, depth), 1) // groups
    ).astype(F32).astype(BF16)
    wide = jnp.dot(low, widen, preferred_element_type=F32)
    block = lax.rem(lax.broadcasted_iota(jnp.int32, (CAP, depth), 1), groups)
    for d in range(groups):
        spread[d * CAP : (d + 1) * CAP, :] = jnp.where(block == d, wide, 0.0).astype(BF16)
    result = jnp.dot(spread[...], up[...], preferred_element_type=F32)
    out[...] = result.astype(BF16)


def base_kernel(groups, tile, slots, *refs):
    where = refs[0]
    pieces = refs[1 : 1 + groups]
    weight, _, partner, own, gathered, held, arrival = refs[1 + groups :]
    me, core = where[0], where[1]
    part = pieces[0].shape[0]
    width = own.shape[1]
    count = width // tile

    def fetch(step):
        half = 1 - core if step < count else core
        start = half * width + (step % count) * tile
        return pltpu.make_async_copy(
            weight.at[:, pl.ds(pl.multiple_of(start, 128), tile)],
            held.at[step % slots],
            arrival.at[step % slots],
        )

    for step in range(slots - 1):
        fetch(step).start()
    for d in range(groups):
        start = pl.multiple_of((me ^ d) * part, part)
        gathered[pl.ds(start, part), :] = pieces[d][...]
    for step in range(2 * count):
        if step + slots - 1 < 2 * count:
            fetch(step + slots - 1).start()
        fetch(step).wait()
        out = partner if step < count else own
        start = (step % count) * tile
        out[:, start : start + tile] = jnp.dot(
            gathered[...], held[step % slots], preferred_element_type=F32
        )


def final_kernel(groups, slots, own, other, arrived, out):
    slot = slots[...]
    rows = slot.shape[1]
    place = (
        slot == lax.broadcasted_iota(jnp.int32, (groups * CAP, rows), 0)
    ).astype(F32).astype(BF16)
    delta = lax.dot_general(
        place, arrived[...], (((0,), (0,)), ((), ())), preferred_element_type=F32
    )
    out[...] = (own[...] + other[...] + delta).astype(BF16)


def few_groups(
    tokens, gate_weight, down_panels, up_panels, adapter_scales, adapter_per_row, storage_index_map
):
    groups = lax.axis_size("rows")
    me = lax.axis_index("rows").astype(jnp.int32)
    core = lax.axis_index("tp").astype(jnp.int32)
    part, depth = tokens.shape
    rows = part * groups
    rank = down_panels.shape[1]
    width = up_panels.shape[-1]
    where = me.reshape(1)
    adapter = adapter_per_row.reshape(1, rows)
    swap = [(0, 1), (1, 0)]

    def to(x, d):
        return lax.ppermute(x, "rows", [(i, i ^ d) for i in range(groups)])

    def params(limit):
        return pltpu.CompilerParams(vmem_limit_bytes=limit << 20)

    slot = pl.pallas_call(
        slots_kernel,
        out_shape=jax.ShapeDtypeStruct((1, rows), jnp.int32),
        in_specs=[SMEM, VMEM],
        out_specs=VMEM,
        compiler_params=params(2),
        cost_estimate=pl.CostEstimate(flops=10**11, bytes_accessed=10**8, transcendentals=0),
        name="slots",
    )(storage_index_map, adapter)

    pieces = {0: tokens}
    for d in range(2, groups, 2):
        pieces[d] = to(tokens, d)
    for d in range(0, groups, 2):
        pieces[d + 1] = to(pieces[d], 1)
    pieces = [pieces[d] for d in range(groups)]

    low = pl.pallas_call(
        functools.partial(lowrank_kernel, groups),
        out_shape=jax.ShapeDtypeStruct((CAP, rank), F32),
        in_specs=[SMEM, VMEM] + [VMEM] * groups + [VMEM],
        out_specs=VMEM,
        scratch_shapes=[pltpu.VMEM((rows, depth), BF16)],
        compiler_params=params(8),
        cost_estimate=pl.CostEstimate(flops=10**8, bytes_accessed=2 * 10**6, transcendentals=0),
        name="lowrank",
    )(where, slot, *pieces, down_panels[0])
    low_other = lax.ppermute(low, "tp", swap)

    deltas = pl.pallas_call(
        functools.partial(delta_kernel, groups),
        out_shape=jax.ShapeDtypeStruct((groups * CAP, width), BF16),
        in_specs=[SMEM, VMEM, VMEM, VMEM],
        out_specs=VMEM,
        scratch_shapes=[pltpu.VMEM((groups * CAP, rank * groups), BF16)],
        compiler_params=params(8),
        cost_estimate=pl.CostEstimate(flops=5 * 10**8, bytes_accessed=3 * 10**6, transcendentals=0),
        name="delta",
    )(adapter_scales, low, low_other, up_panels.reshape(rank * groups, width))
    arrived = lax.all_to_all(deltas, "rows", split_axis=0, concat_axis=0, tiled=True)

    tile, buffers = 256, 5
    half = jax.ShapeDtypeStruct((rows, width), F32)
    partner, own = pl.pallas_call(
        functools.partial(base_kernel, groups, tile, buffers),
        in_specs=[SMEM] + [VMEM] * groups + [ANY, ANY],
        out_specs=[VMEM, VMEM],
        scratch_shapes=[
            pltpu.VMEM((rows, depth), BF16),
            pltpu.VMEM((buffers, depth, tile), BF16),
            pltpu.SemaphoreType.DMA((buffers,)),
        ],
        out_shape=[half, half],
        compiler_params=params(40),
        cost_estimate=pl.CostEstimate(
            flops=4 * rows * depth * width, bytes_accessed=10**7, transcendentals=0
        ),
        name="base",
    )(jnp.stack([me, core]), *pieces, gate_weight, deltas)
    other = lax.ppermute(partner, "tp", swap)

    return pl.pallas_call(
        functools.partial(final_kernel, groups),
        out_shape=jax.ShapeDtypeStruct((rows, width), BF16),
        in_specs=[VMEM, VMEM, VMEM, VMEM],
        out_specs=VMEM,
        compiler_params=params(8),
        cost_estimate=pl.CostEstimate(flops=2 * 10**8, bytes_accessed=4 * 10**6, transcendentals=0),
        name="combine",
    )(slot, own, other, arrived)


def on_device(*args):
    if lax.axis_size("rows") in (2, 4, 8):
        return few_groups(*args)
    return many_groups(*args)


def solution(mesh):
    placed = (
        P(("parts", "rows"), "tp"),
        P("tp", "rows"),
        P("rows", None, "tp"),
        P("rows", None, None, "tp", None),
        P("rows"),
        P("parts", None),
        P(),
    )
    return jax.shard_map(
        on_device, mesh=mesh, in_specs=placed, out_specs=P("parts", ("rows", "tp")), check_vma=False
    )
```

```python
import functools

import jax
import jax.numpy as jnp
from jax import lax
from jax.experimental import pallas as pl
from jax.experimental.pallas import tpu as pltpu
from jax.sharding import PartitionSpec as P

CAP = 32
F32 = jnp.float32
BF16 = jnp.bfloat16
VMEM = pl.BlockSpec(memory_space=pltpu.VMEM)
SMEM = pl.BlockSpec(memory_space=pltpu.SMEM)
ANY = pl.BlockSpec(memory_space=pl.ANY)


def slot_layout(adapter_per_row, storage_index_map, owner_indices, slot_depth):
    row_total = adapter_per_row.shape[0]
    stored = jnp.take(storage_index_map, adapter_per_row[:, 0], axis=0)
    row_order = jnp.argsort(stored, stable=True)
    arranged = jnp.take(stored, row_order, axis=0)
    matches = (stored[:, None] == jnp.arange(owner_indices, dtype=jnp.int32)[None, :]).astype(
        jnp.int32
    )
    counts = jnp.sum(matches, axis=0)
    starts = jnp.cumsum(counts) - counts
    within = jnp.arange(row_total, dtype=jnp.int32) - jnp.take(starts, arranged, axis=0)
    placed = arranged * slot_depth + within
    slot_of_row = jnp.zeros((row_total,), jnp.int32).at[row_order].set(placed)
    row_of_slot = (
        jnp.full((owner_indices * slot_depth,), row_total, jnp.int32)
        .at[slot_of_row]
        .set(jnp.arange(row_total, dtype=jnp.int32))
    )
    return (slot_of_row, row_of_slot)


def many_groups(
    tokens, gate_weight, down_panels, up_panels, adapter_scales, adapter_per_row, storage_index_map
):
    owner_indices = lax.axis_size("rows")
    myself = lax.axis_index("rows")
    slot_of_row, row_of_slot = slot_layout(adapter_per_row, storage_index_map, owner_indices, CAP)
    my_rows = lax.dynamic_slice_in_dim(row_of_slot, myself * CAP, CAP, 0)
    piece = lax.all_gather(tokens, "rows", axis=0, tiled=True)
    inside = my_rows < piece.shape[0]
    taken = jnp.take(piece, jnp.clip(my_rows, 0, piece.shape[0] - 1), axis=0)
    selected = jnp.where(inside[:, None], taken, jnp.zeros_like(taken))
    block = jnp.dot(piece, gate_weight, preferred_element_type=F32)
    halves = lax.psum_scatter(block, "tp", scatter_dimension=1, tiled=True)
    width = up_panels.shape[-1]
    low = lax.dot_general(
        selected, down_panels[0], (((1,), (1,)), ((), ())), preferred_element_type=F32
    )
    low = low + lax.ppermute(low, "tp", [(0, 1), (1, 0)])
    low = (low * adapter_scales[0]).astype(BF16)
    panel = up_panels.reshape(down_panels.shape[1], owner_indices, width)
    delta = jnp.einsum("cr,rof->ocf", low, panel, preferred_element_type=F32).astype(BF16)
    arrived = lax.all_to_all(delta, "rows", split_axis=0, concat_axis=0, tiled=True)
    delta_rows = jnp.take(arrived.reshape(owner_indices * CAP, width), slot_of_row, axis=0)
    return (halves + delta_rows.astype(F32)).astype(BF16)


def slots_as_row(adapter_ref, map_ref):
    rows = adapter_ref.shape[1]
    count = map_ref.shape[0]
    adapter = adapter_ref[...]
    stored = jnp.zeros_like(adapter)
    for a in range(count):
        stored = jnp.where(adapter == a, map_ref[a], stored)
    index = lax.broadcasted_iota(jnp.int32, (count, rows), 0)
    match = (stored == index).astype(F32)
    earlier = (
        lax.broadcasted_iota(jnp.int32, (rows, rows), 0)
        < lax.broadcasted_iota(jnp.int32, (rows, rows), 1)
    ).astype(F32)
    before = jnp.dot(match.astype(BF16), earlier.astype(BF16), preferred_element_type=F32)
    within = jnp.sum(match * before, axis=0, keepdims=True)
    return stored * CAP + within.astype(jnp.int32)


def slots_kernel(where, index_map, adapter, weight, slot, ahead, arrival):
    width = weight.shape[1] // 2
    start = pl.multiple_of((1 - where[1]) * width, 128)
    copy = pltpu.make_async_copy(weight.at[:, pl.ds(start, ahead.shape[1])], ahead, arrival.at[0])
    copy.start()
    slot[...] = slots_as_row(adapter, index_map)
    copy.wait()


def lowrank_kernel(groups, *refs):
    where, slots = refs[:2]
    pieces = refs[2 : 2 + groups]
    down, out, gathered = refs[2 + groups :]
    me = where[0]
    part = pieces[0].shape[0]
    for d in range(groups):
        start = pl.multiple_of((me ^ d) * part, part)
        gathered[pl.ds(start, part), :] = pieces[d][...]
    slot = slots[...]
    rows = slot.shape[1]
    mine = lax.broadcasted_iota(jnp.int32, (CAP, rows), 0) + me * CAP
    chosen = (slot == mine).astype(F32).astype(BF16)
    selected = jnp.dot(chosen, gathered[...], preferred_element_type=F32).astype(BF16)
    out[...] = lax.dot_general(
        selected, down[...], (((1,), (1,)), ((), ())), preferred_element_type=F32
    )


def delta_kernel(groups, offsets, where, scale, low_a, low_b, up, _, *refs):
    outs, spread = refs[:-1], refs[-1]
    me = where[0]
    rank = low_a.shape[1]
    low = ((low_a[...] + low_b[...]) * scale[0]).astype(BF16)
    depth = rank * groups
    widen = (
        lax.broadcasted_iota(jnp.int32, (rank, depth), 0)
        == lax.broadcasted_iota(jnp.int32, (rank, depth), 1) // groups
    ).astype(F32).astype(BF16)
    wide = jnp.dot(low, widen, preferred_element_type=F32)
    block = lax.rem(lax.broadcasted_iota(jnp.int32, (CAP, depth), 1), groups)
    for i, d in enumerate(offsets):
        spread[i * CAP : (i + 1) * CAP, :] = jnp.where(block == (me ^ d), wide, 0.0).astype(BF16)
    result = jnp.dot(spread[...], up[...], preferred_element_type=F32).astype(BF16)
    for i, out in enumerate(outs):
        out[...] = result[i * CAP : (i + 1) * CAP, :]


def base_kernel(groups, *refs):
    where = refs[0]
    pieces = refs[1 : 1 + groups]
    ahead, weight, _, _, partner, own, gathered, held, arrival = refs[1 + groups :]
    me, core = where[0], where[1]
    part = pieces[0].shape[0]
    width = own.shape[1]
    slots, _, tile = held.shape
    ready = ahead.shape[1] // tile
    count = width // tile
    last = 2 * count

    def fetch(step):
        half = 1 - core if step < count else core
        start = half * width + (step % count) * tile
        return pltpu.make_async_copy(
            weight.at[:, pl.ds(pl.multiple_of(start, 128), tile)],
            held.at[step % slots],
            arrival.at[step % slots],
        )

    for step in range(ready, ready + slots - 1):
        fetch(step).start()
    for d in range(groups):
        start = pl.multiple_of((me ^ d) * part, part)
        gathered[pl.ds(start, part), :] = pieces[d][...]
    for step in range(last):
        if step < ready:
            columns = ahead[:, step * tile : (step + 1) * tile]
        else:
            if step + slots - 1 < last:
                fetch(step + slots - 1).start()
            fetch(step).wait()
            columns = held[step % slots]
        out = partner if step < count else own
        start = (step % count) * tile
        out[:, start : start + tile] = jnp.dot(
            gathered[...], columns, preferred_element_type=F32
        )


def place_kernel(slots, place):
    place[...] = (
        slots[...] == lax.broadcasted_iota(jnp.int32, place.shape, 0)
    ).astype(F32).astype(BF16)


def final_kernel(groups, where, place, own, other, *refs):
    pieces, out, arrived = refs[:groups], refs[-2], refs[-1]
    me = where[0]
    for d in range(groups):
        start = pl.multiple_of((me ^ d) * CAP, CAP)
        arrived[pl.ds(start, CAP), :] = pieces[d][...]
    delta = lax.dot_general(
        place[...], arrived[...], (((0,), (0,)), ((), ())), preferred_element_type=F32
    )
    out[...] = (own[...] + other[...] + delta).astype(BF16)


def few_groups(
    tokens, gate_weight, down_panels, up_panels, adapter_scales, adapter_per_row, storage_index_map
):
    groups = lax.axis_size("rows")
    me = lax.axis_index("rows").astype(jnp.int32)
    core = lax.axis_index("tp").astype(jnp.int32)
    part, depth = tokens.shape
    rows = part * groups
    rank = down_panels.shape[1]
    width = up_panels.shape[-1]
    where = me.reshape(1)
    adapter = adapter_per_row.reshape(1, rows)
    swap = [(0, 1), (1, 0)]

    def to(x, d):
        return lax.ppermute(x, "rows", [(i, i ^ d) for i in range(groups)])

    def params(limit):
        return pltpu.CompilerParams(vmem_limit_bytes=limit << 20)

    tile, buffers, ready = 256, 5, 4
    both = jnp.stack([me, core])
    slot, ahead = pl.pallas_call(
        slots_kernel,
        out_shape=[
            jax.ShapeDtypeStruct((1, rows), jnp.int32),
            jax.ShapeDtypeStruct((depth, ready * tile), BF16),
        ],
        in_specs=[SMEM, SMEM, VMEM, ANY],
        out_specs=[VMEM, VMEM],
        scratch_shapes=[pltpu.SemaphoreType.DMA((1,))],
        compiler_params=params(37),
        cost_estimate=pl.CostEstimate(flops=10**11, bytes_accessed=10**8, transcendentals=0),
        name="slots",
    )(both, storage_index_map, adapter, gate_weight)

    pieces = {0: tokens}
    steps = [1 << i for i in range(groups.bit_length() - 1)]
    for d in reversed(steps):
        pieces[d] = to(tokens, d)
    if groups > 2:
        pieces[groups - 1] = to(tokens, groups - 1)
    for d in range(1, groups):
        if d not in pieces:
            far = max(step for step in steps if step <= d)
            pieces[d] = to(pieces[far], d - far)
    pieces = [pieces[d] for d in range(groups)]

    low = pl.pallas_call(
        functools.partial(lowrank_kernel, groups),
        out_shape=jax.ShapeDtypeStruct((CAP, rank), F32),
        in_specs=[SMEM, VMEM] + [VMEM] * groups + [VMEM],
        out_specs=VMEM,
        scratch_shapes=[pltpu.VMEM((rows, depth), BF16)],
        compiler_params=params(8),
        cost_estimate=pl.CostEstimate(flops=10**8, bytes_accessed=2 * 10**6, transcendentals=0),
        name="lowrank",
    )(where, slot, *pieces, down_panels[0])
    low_other = lax.ppermute(low, "tp", swap)

    up = up_panels.reshape(rank * groups, width)

    def deltas(offsets, after):
        return pl.pallas_call(
            functools.partial(delta_kernel, groups, offsets),
            out_shape=[jax.ShapeDtypeStruct((CAP, width), BF16)] * len(offsets),
            in_specs=[SMEM, SMEM, VMEM, VMEM, VMEM, ANY],
            out_specs=[VMEM] * len(offsets),
            scratch_shapes=[pltpu.VMEM((len(offsets) * CAP, rank * groups), BF16)],
            compiler_params=params(8),
            cost_estimate=pl.CostEstimate(flops=10**6, bytes_accessed=10**6, transcendentals=0),
            name="delta",
        )(where, adapter_scales, low, low_other, up, after)

    arrived = [None] * groups
    blocks = deltas((0, 2, 1, 4, 5, 6), low)
    for d, x in zip((0, 2, 1, 4, 5, 6), blocks):
        arrived[d] = to(x, d) if d else x
    seventh = deltas((7,), arrived[1])[0]
    arrived[7] = to(seventh, 7)
    eighth = deltas((3,), arrived[2])[0]
    arrived[3] = to(eighth, 3)

    half = jax.ShapeDtypeStruct((rows, width), F32)
    partner, own = pl.pallas_call(
        functools.partial(base_kernel, groups),
        in_specs=[SMEM] + [VMEM] * groups + [VMEM, ANY, ANY, ANY],
        out_specs=[VMEM, VMEM],
        scratch_shapes=[
            pltpu.VMEM((rows, depth), BF16),
            pltpu.VMEM((buffers, depth, tile), BF16),
            pltpu.SemaphoreType.DMA((buffers,)),
        ],
        out_shape=[half, half],
        compiler_params=params(37),
        cost_estimate=pl.CostEstimate(
            flops=4 * rows * depth * width, bytes_accessed=10**7, transcendentals=0
        ),
        name="base",
    )(both, *pieces, ahead, gate_weight, seventh, eighth)
    other = lax.ppermute(partner, "tp", swap)

    place = pl.pallas_call(
        place_kernel,
        out_shape=jax.ShapeDtypeStruct((groups * CAP, rows), BF16),
        in_specs=[VMEM],
        out_specs=VMEM,
        compiler_params=params(2),
        cost_estimate=pl.CostEstimate(flops=10**11, bytes_accessed=10**8, transcendentals=0),
        name="place",
    )(slot)

    return pl.pallas_call(
        functools.partial(final_kernel, groups),
        out_shape=jax.ShapeDtypeStruct((rows, width), BF16),
        in_specs=[SMEM, VMEM, VMEM, VMEM] + [VMEM] * groups,
        out_specs=VMEM,
        scratch_shapes=[pltpu.VMEM((groups * CAP, width), BF16)],
        compiler_params=params(8),
        cost_estimate=pl.CostEstimate(flops=2 * 10**8, bytes_accessed=4 * 10**6, transcendentals=0),
        name="combine",
    )(where, place, own, other, *arrived)


def on_device(*args):
    if lax.axis_size("rows") == 8:
        return few_groups(*args)
    return many_groups(*args)


def solution(mesh):
    placed = (
        P(("parts", "rows"), "tp"),
        P("tp", "rows"),
        P("rows", None, "tp"),
        P("rows", None, None, "tp", None),
        P("rows"),
        P("parts", None),
        P(),
    )
    return jax.shard_map(
        on_device, mesh=mesh, in_specs=placed, out_specs=P("parts", ("rows", "tp")), check_vma=False
    )
```

```python
import functools

import jax
import jax.numpy as jnp
from jax import lax
from jax.experimental import pallas as pl
from jax.experimental.pallas import tpu as pltpu
from jax.sharding import PartitionSpec as P

CAP = 32
F32 = jnp.float32
BF16 = jnp.bfloat16
VMEM = pl.BlockSpec(memory_space=pltpu.VMEM)
SMEM = pl.BlockSpec(memory_space=pltpu.SMEM)
ANY = pl.BlockSpec(memory_space=pl.ANY)


def slot_layout(adapter_per_row, storage_index_map, owner_indices, slot_depth):
    row_total = adapter_per_row.shape[0]
    stored = jnp.take(storage_index_map, adapter_per_row[:, 0], axis=0)
    row_order = jnp.argsort(stored, stable=True)
    arranged = jnp.take(stored, row_order, axis=0)
    matches = (stored[:, None] == jnp.arange(owner_indices, dtype=jnp.int32)[None, :]).astype(
        jnp.int32
    )
    counts = jnp.sum(matches, axis=0)
    starts = jnp.cumsum(counts) - counts
    within = jnp.arange(row_total, dtype=jnp.int32) - jnp.take(starts, arranged, axis=0)
    placed = arranged * slot_depth + within
    slot_of_row = jnp.zeros((row_total,), jnp.int32).at[row_order].set(placed)
    row_of_slot = (
        jnp.full((owner_indices * slot_depth,), row_total, jnp.int32)
        .at[slot_of_row]
        .set(jnp.arange(row_total, dtype=jnp.int32))
    )
    return (slot_of_row, row_of_slot)


def many_groups(
    tokens, gate_weight, down_panels, up_panels, adapter_scales, adapter_per_row, storage_index_map
):
    owner_indices = lax.axis_size("rows")
    myself = lax.axis_index("rows")
    slot_of_row, row_of_slot = slot_layout(adapter_per_row, storage_index_map, owner_indices, CAP)
    my_rows = lax.dynamic_slice_in_dim(row_of_slot, myself * CAP, CAP, 0)
    piece = lax.all_gather(tokens, "rows", axis=0, tiled=True)
    inside = my_rows < piece.shape[0]
    taken = jnp.take(piece, jnp.clip(my_rows, 0, piece.shape[0] - 1), axis=0)
    selected = jnp.where(inside[:, None], taken, jnp.zeros_like(taken))
    block = jnp.dot(piece, gate_weight, preferred_element_type=F32)
    halves = lax.psum_scatter(block, "tp", scatter_dimension=1, tiled=True)
    width = up_panels.shape[-1]
    low = lax.dot_general(
        selected, down_panels[0], (((1,), (1,)), ((), ())), preferred_element_type=F32
    )
    low = low + lax.ppermute(low, "tp", [(0, 1), (1, 0)])
    low = (low * adapter_scales[0]).astype(BF16)
    panel = up_panels.reshape(down_panels.shape[1], owner_indices, width)
    delta = jnp.einsum("cr,rof->ocf", low, panel, preferred_element_type=F32).astype(BF16)
    arrived = lax.all_to_all(delta, "rows", split_axis=0, concat_axis=0, tiled=True)
    delta_rows = jnp.take(arrived.reshape(owner_indices * CAP, width), slot_of_row, axis=0)
    return (halves + delta_rows.astype(F32)).astype(BF16)


def slots_as_row(adapter_ref, map_ref):
    rows = adapter_ref.shape[1]
    count = map_ref.shape[0]
    adapter = adapter_ref[...]
    stored = jnp.zeros_like(adapter)
    for a in range(count):
        stored = jnp.where(adapter == a, map_ref[a], stored)
    index = lax.broadcasted_iota(jnp.int32, (count, rows), 0)
    match = (stored == index).astype(F32)
    earlier = (
        lax.broadcasted_iota(jnp.int32, (rows, rows), 0)
        < lax.broadcasted_iota(jnp.int32, (rows, rows), 1)
    ).astype(F32)
    before = jnp.dot(match.astype(BF16), earlier.astype(BF16), preferred_element_type=F32)
    within = jnp.sum(match * before, axis=0, keepdims=True)
    return stored * CAP + within.astype(jnp.int32)


def slots_kernel(where, index_map, adapter, weight, slot, ahead, arrival):
    width = weight.shape[1] // 2
    start = pl.multiple_of((1 - where[1]) * width, 128)
    copy = pltpu.make_async_copy(weight.at[:, pl.ds(start, ahead.shape[1])], ahead, arrival.at[0])
    copy.start()
    slot[...] = slots_as_row(adapter, index_map)
    copy.wait()


def lowrank_kernel(groups, *refs):
    where, slots = refs[:2]
    pieces = refs[2 : 2 + groups]
    down, out, gathered = refs[2 + groups :]
    me = where[0]
    part = pieces[0].shape[0]
    for d in range(groups):
        start = pl.multiple_of((me ^ d) * part, part)
        gathered[pl.ds(start, part), :] = pieces[d][...]
    slot = slots[...]
    rows = slot.shape[1]
    mine = lax.broadcasted_iota(jnp.int32, (CAP, rows), 0) + me * CAP
    chosen = (slot == mine).astype(F32).astype(BF16)
    selected = jnp.dot(chosen, gathered[...], preferred_element_type=F32).astype(BF16)
    out[...] = lax.dot_general(
        selected, down[...], (((1,), (1,)), ((), ())), preferred_element_type=F32
    )


def relay_kernel(block, _, out):
    out[...] = block[...]


def delta_kernel(groups, offsets, where, scale, low_a, low_b, up, _, *refs):
    outs, spread = refs[:-1], refs[-1]
    me = where[0]
    rank = low_a.shape[1]
    low = ((low_a[...] + low_b[...]) * scale[...]).astype(BF16)
    depth = rank * groups
    widen = (
        lax.broadcasted_iota(jnp.int32, (rank, depth), 0)
        == lax.broadcasted_iota(jnp.int32, (rank, depth), 1) // groups
    ).astype(F32).astype(BF16)
    wide = jnp.dot(low, widen, preferred_element_type=F32)
    block = lax.rem(lax.broadcasted_iota(jnp.int32, (CAP, depth), 1), groups)
    for i, d in enumerate(offsets):
        spread[i * CAP : (i + 1) * CAP, :] = jnp.where(block == (me ^ d), wide, 0.0).astype(BF16)
    result = jnp.dot(spread[...], up[...], preferred_element_type=F32).astype(BF16)
    for i, out in enumerate(outs):
        out[...] = result[i * CAP : (i + 1) * CAP, :]


def base_kernel(groups, *refs):
    where = refs[0]
    pieces = refs[1 : 1 + groups]
    ahead, weight, _, _, partner, own, gathered, held, arrival = refs[1 + groups :]
    me, core = where[0], where[1]
    part = pieces[0].shape[0]
    width = own.shape[1]
    slots, _, tile = held.shape
    ready = ahead.shape[1] // tile
    count = width // tile
    last = 2 * count

    def fetch(step):
        half = 1 - core if step < count else core
        start = half * width + (step % count) * tile
        return pltpu.make_async_copy(
            weight.at[:, pl.ds(pl.multiple_of(start, 128), tile)],
            held.at[step % slots],
            arrival.at[step % slots],
        )

    for step in range(ready, ready + slots - 1):
        fetch(step).start()
    for d in range(groups):
        start = pl.multiple_of((me ^ d) * part, part)
        gathered[pl.ds(start, part), :] = pieces[d][...]
    for step in range(last):
        if step < ready:
            columns = ahead[:, step * tile : (step + 1) * tile]
        else:
            if step + slots - 1 < last:
                fetch(step + slots - 1).start()
            fetch(step).wait()
            columns = held[step % slots]
        out = partner if step < count else own
        start = (step % count) * tile
        out[:, start : start + tile] = jnp.dot(
            gathered[...], columns, preferred_element_type=F32
        )


def place_kernel(slots, place):
    place[...] = (
        slots[...] == lax.broadcasted_iota(jnp.int32, place.shape, 0)
    ).astype(F32).astype(BF16)


def final_kernel(groups, where, place, own, other, *refs):
    pieces, out, arrived = refs[:groups], refs[-2], refs[-1]
    me = where[0]
    for d in range(groups):
        start = pl.multiple_of((me ^ d) * CAP, CAP)
        arrived[pl.ds(start, CAP), :] = pieces[d][...]
    delta = lax.dot_general(
        place[...], arrived[...], (((0,), (0,)), ((), ())), preferred_element_type=F32
    )
    out[...] = (own[...] + other[...] + delta).astype(BF16)


def few_groups(
    tokens, gate_weight, down_panels, up_panels, adapter_scales, adapter_per_row, storage_index_map
):
    groups = lax.axis_size("rows")
    me = lax.axis_index("rows").astype(jnp.int32)
    core = lax.axis_index("tp").astype(jnp.int32)
    part, depth = tokens.shape
    rows = part * groups
    rank = down_panels.shape[1]
    width = up_panels.shape[-1]
    where = me.reshape(1)
    adapter = adapter_per_row.reshape(1, rows)
    swap = [(0, 1), (1, 0)]

    def to(x, d):
        return lax.ppermute(x, "rows", [(i, i ^ d) for i in range(groups)])

    def params(limit):
        return pltpu.CompilerParams(vmem_limit_bytes=limit << 20)

    tile, buffers, ready = 256, 5, 4
    both = jnp.stack([me, core])
    slot, ahead = pl.pallas_call(
        slots_kernel,
        out_shape=[
            jax.ShapeDtypeStruct((1, rows), jnp.int32),
            jax.ShapeDtypeStruct((depth, ready * tile), BF16),
        ],
        in_specs=[SMEM, SMEM, VMEM, ANY],
        out_specs=[VMEM, VMEM],
        scratch_shapes=[pltpu.SemaphoreType.DMA((1,))],
        compiler_params=params(37),
        cost_estimate=pl.CostEstimate(flops=10**11, bytes_accessed=10**8, transcendentals=0),
        name="slots",
    )(both, storage_index_map, adapter, gate_weight)

    pieces = {0: tokens}
    steps = [1 << i for i in range(groups.bit_length() - 1)]
    for d in reversed(steps):
        pieces[d] = to(tokens, d)
    if groups > 2:
        pieces[groups - 1] = to(tokens, groups - 1)
    for d in range(1, groups):
        if d not in pieces:
            far = max(step for step in steps if step <= d)
            pieces[d] = to(pieces[far], d - far)
    pieces = [pieces[d] for d in range(groups)]

    low = pl.pallas_call(
        functools.partial(lowrank_kernel, groups),
        out_shape=jax.ShapeDtypeStruct((CAP, rank), F32),
        in_specs=[SMEM, VMEM] + [VMEM] * groups + [VMEM],
        out_specs=VMEM,
        scratch_shapes=[pltpu.VMEM((rows, depth), BF16)],
        compiler_params=params(8),
        cost_estimate=pl.CostEstimate(flops=10**8, bytes_accessed=2 * 10**6, transcendentals=0),
        name="lowrank",
    )(where, slot, *pieces, down_panels[0])
    low_other = lax.ppermute(low, "tp", swap)

    up = up_panels.reshape(rank * groups, width)

    def deltas(offsets, after):
        return pl.pallas_call(
            functools.partial(delta_kernel, groups, offsets),
            out_shape=[jax.ShapeDtypeStruct((CAP, width), BF16)] * len(offsets),
            in_specs=[SMEM, VMEM, VMEM, VMEM, VMEM, ANY],
            out_specs=[VMEM] * len(offsets),
            scratch_shapes=[pltpu.VMEM((len(offsets) * CAP, rank * groups), BF16)],
            compiler_params=params(8),
            cost_estimate=pl.CostEstimate(flops=10**6, bytes_accessed=10**6, transcendentals=0),
            name="delta",
        )(where, adapter_scales.reshape(1, 1), low, low_other, up, after)

    arrived = [None] * groups
    order = (0, 2, 1, 4, 5, 6, 7, 3)
    blocks = deltas(order, low)
    for d, x in zip(order[:6], blocks):
        arrived[d] = to(x, d) if d else x

    def once(block, after):
        return pl.pallas_call(
            relay_kernel,
            out_shape=jax.ShapeDtypeStruct(block.shape, block.dtype),
            in_specs=[VMEM, ANY],
            out_specs=VMEM,
            compiler_params=params(2),
            cost_estimate=pl.CostEstimate(flops=10**4, bytes_accessed=10**4, transcendentals=0),
            name="relay",
        )(block, after)

    seventh = once(blocks[6], arrived[1])
    arrived[7] = to(seventh, 7)
    eighth = once(blocks[7], arrived[2])
    arrived[3] = to(eighth, 3)

    half = jax.ShapeDtypeStruct((rows, width), F32)
    partner, own = pl.pallas_call(
        functools.partial(base_kernel, groups),
        in_specs=[SMEM] + [VMEM] * groups + [VMEM, ANY, ANY, ANY],
        out_specs=[VMEM, VMEM],
        scratch_shapes=[
            pltpu.VMEM((rows, depth), BF16),
            pltpu.VMEM((buffers, depth, tile), BF16),
            pltpu.SemaphoreType.DMA((buffers,)),
        ],
        out_shape=[half, half],
        compiler_params=params(37),
        cost_estimate=pl.CostEstimate(
            flops=4 * rows * depth * width, bytes_accessed=10**7, transcendentals=0
        ),
        name="base",
    )(both, *pieces, ahead, gate_weight, seventh, eighth)
    other = lax.ppermute(partner, "tp", swap)

    place = pl.pallas_call(
        place_kernel,
        out_shape=jax.ShapeDtypeStruct((groups * CAP, rows), BF16),
        in_specs=[VMEM],
        out_specs=VMEM,
        compiler_params=params(2),
        cost_estimate=pl.CostEstimate(flops=10**11, bytes_accessed=10**8, transcendentals=0),
        name="place",
    )(slot)

    return pl.pallas_call(
        functools.partial(final_kernel, groups),
        out_shape=jax.ShapeDtypeStruct((rows, width), BF16),
        in_specs=[SMEM, VMEM, VMEM, VMEM] + [VMEM] * groups,
        out_specs=VMEM,
        scratch_shapes=[pltpu.VMEM((groups * CAP, width), BF16)],
        compiler_params=params(8),
        cost_estimate=pl.CostEstimate(flops=2 * 10**8, bytes_accessed=4 * 10**6, transcendentals=0),
        name="combine",
    )(where, place, own, other, *arrived)


def on_device(*args):
    if lax.axis_size("rows") == 8:
        return few_groups(*args)
    return many_groups(*args)


def solution(mesh):
    placed = (
        P(("parts", "rows"), "tp"),
        P("tp", "rows"),
        P("rows", None, "tp"),
        P("rows", None, None, "tp", None),
        P("rows"),
        P("parts", None),
        P(),
    )
    return jax.shard_map(
        on_device, mesh=mesh, in_specs=placed, out_specs=P("parts", ("rows", "tp")), check_vma=False
    )
```

```python
import functools

import jax
import jax.numpy as jnp
from jax import lax
from jax.experimental import pallas as pl
from jax.experimental.pallas import tpu as pltpu
from jax.sharding import PartitionSpec as P

CAP = 32
F32 = jnp.float32
BF16 = jnp.bfloat16
VMEM = pl.BlockSpec(memory_space=pltpu.VMEM)
SMEM = pl.BlockSpec(memory_space=pltpu.SMEM)
ANY = pl.BlockSpec(memory_space=pl.ANY)


def slot_layout(adapter_per_row, storage_index_map, owner_indices, slot_depth):
    row_total = adapter_per_row.shape[0]
    stored = jnp.take(storage_index_map, adapter_per_row[:, 0], axis=0)
    row_order = jnp.argsort(stored, stable=True)
    arranged = jnp.take(stored, row_order, axis=0)
    matches = (stored[:, None] == jnp.arange(owner_indices, dtype=jnp.int32)[None, :]).astype(
        jnp.int32
    )
    counts = jnp.sum(matches, axis=0)
    starts = jnp.cumsum(counts) - counts
    within = jnp.arange(row_total, dtype=jnp.int32) - jnp.take(starts, arranged, axis=0)
    placed = arranged * slot_depth + within
    slot_of_row = jnp.zeros((row_total,), jnp.int32).at[row_order].set(placed)
    row_of_slot = (
        jnp.full((owner_indices * slot_depth,), row_total, jnp.int32)
        .at[slot_of_row]
        .set(jnp.arange(row_total, dtype=jnp.int32))
    )
    return (slot_of_row, row_of_slot)


def many_groups(
    tokens, gate_weight, down_panels, up_panels, adapter_scales, adapter_per_row, storage_index_map
):
    owner_indices = lax.axis_size("rows")
    myself = lax.axis_index("rows")
    slot_of_row, row_of_slot = slot_layout(adapter_per_row, storage_index_map, owner_indices, CAP)
    my_rows = lax.dynamic_slice_in_dim(row_of_slot, myself * CAP, CAP, 0)
    piece = lax.all_gather(tokens, "rows", axis=0, tiled=True)
    inside = my_rows < piece.shape[0]
    taken = jnp.take(piece, jnp.clip(my_rows, 0, piece.shape[0] - 1), axis=0)
    selected = jnp.where(inside[:, None], taken, jnp.zeros_like(taken))
    block = jnp.dot(piece, gate_weight, preferred_element_type=F32)
    halves = lax.psum_scatter(block, "tp", scatter_dimension=1, tiled=True)
    width = up_panels.shape[-1]
    low = lax.dot_general(
        selected, down_panels[0], (((1,), (1,)), ((), ())), preferred_element_type=F32
    )
    low = low + lax.ppermute(low, "tp", [(0, 1), (1, 0)])
    low = (low * adapter_scales[0]).astype(BF16)
    panel = up_panels.reshape(down_panels.shape[1], owner_indices, width)
    delta = jnp.einsum("cr,rof->ocf", low, panel, preferred_element_type=F32).astype(BF16)
    arrived = lax.all_to_all(delta, "rows", split_axis=0, concat_axis=0, tiled=True)
    delta_rows = jnp.take(arrived.reshape(owner_indices * CAP, width), slot_of_row, axis=0)
    return (halves + delta_rows.astype(F32)).astype(BF16)


def slots_as_row(adapter_ref, map_ref):
    rows = adapter_ref.shape[1]
    count = map_ref.shape[0]
    adapter = adapter_ref[...]
    stored = jnp.zeros_like(adapter)
    for a in range(count):
        stored = jnp.where(adapter == a, map_ref[a], stored)
    index = lax.broadcasted_iota(jnp.int32, (count, rows), 0)
    match = (stored == index).astype(F32)
    earlier = (
        lax.broadcasted_iota(jnp.int32, (rows, rows), 0)
        < lax.broadcasted_iota(jnp.int32, (rows, rows), 1)
    ).astype(F32)
    before = jnp.dot(match.astype(BF16), earlier.astype(BF16), preferred_element_type=F32)
    within = jnp.sum(match * before, axis=0, keepdims=True)
    return stored * CAP + within.astype(jnp.int32)


def slots_kernel(where, index_map, adapter, weight, slot, ahead, arrival):
    width = weight.shape[1] // 2
    start = pl.multiple_of((1 - where[1]) * width, 128)
    copy = pltpu.make_async_copy(weight.at[:, pl.ds(start, ahead.shape[1])], ahead, arrival.at[0])
    copy.start()
    slot[...] = slots_as_row(adapter, index_map)
    copy.wait()


def lowrank_kernel(groups, *refs):
    where, slots = refs[:2]
    pieces = refs[2 : 2 + groups]
    down, out, gathered = refs[2 + groups :]
    me = where[0]
    part = pieces[0].shape[0]
    for d in range(groups):
        start = pl.multiple_of((me ^ d) * part, part)
        gathered[pl.ds(start, part), :] = pieces[d][...]
    slot = slots[...]
    rows = slot.shape[1]
    mine = lax.broadcasted_iota(jnp.int32, (CAP, rows), 0) + me * CAP
    chosen = (slot == mine).astype(F32).astype(BF16)
    selected = jnp.dot(chosen, gathered[...], preferred_element_type=F32).astype(BF16)
    out[...] = lax.dot_general(
        selected, down[...], (((1,), (1,)), ((), ())), preferred_element_type=F32
    )


def relay_kernel(block, _, out):
    out[...] = block[...]


def delta_kernel(groups, offsets, where, scale, low_a, low_b, up, _, *refs):
    outs, spread = refs[:-1], refs[-1]
    me = where[0]
    rank = low_a.shape[1]
    low = ((low_a[...] + low_b[...]) * scale[...]).astype(BF16)
    depth = rank * groups
    widen = (
        lax.broadcasted_iota(jnp.int32, (rank, depth), 0)
        == lax.broadcasted_iota(jnp.int32, (rank, depth), 1) // groups
    ).astype(F32).astype(BF16)
    wide = jnp.dot(low, widen, preferred_element_type=F32)
    block = lax.rem(lax.broadcasted_iota(jnp.int32, (CAP, depth), 1), groups)
    for i, d in enumerate(offsets):
        spread[i * CAP : (i + 1) * CAP, :] = jnp.where(block == (me ^ d), wide, 0.0).astype(BF16)
    result = jnp.dot(spread[...], up[...], preferred_element_type=F32).astype(BF16)
    for i, out in enumerate(outs):
        out[...] = result[i * CAP : (i + 1) * CAP, :]


def base_kernel(groups, *refs):
    where = refs[0]
    pieces = refs[1 : 1 + groups]
    ahead, weight, _, _, partner, own, gathered, held, arrival = refs[1 + groups :]
    me, core = where[0], where[1]
    part = pieces[0].shape[0]
    width = own.shape[1]
    slots, _, tile = held.shape
    ready = ahead.shape[1] // tile
    count = width // tile
    last = 2 * count

    def fetch(step):
        half = 1 - core if step < count else core
        start = half * width + (step % count) * tile
        return pltpu.make_async_copy(
            weight.at[:, pl.ds(pl.multiple_of(start, 128), tile)],
            held.at[step % slots],
            arrival.at[step % slots],
        )

    for step in range(ready, ready + slots - 1):
        fetch(step).start()
    for d in range(groups):
        start = pl.multiple_of((me ^ d) * part, part)
        gathered[pl.ds(start, part), :] = pieces[d][...]
    for step in range(last):
        if step < ready:
            columns = ahead[:, step * tile : (step + 1) * tile]
        else:
            if step + slots - 1 < last:
                fetch(step + slots - 1).start()
            fetch(step).wait()
            columns = held[step % slots]
        out = partner if step < count else own
        start = (step % count) * tile
        out[:, start : start + tile] = jnp.dot(
            gathered[...], columns, preferred_element_type=F32
        )


def place_kernel(slots, place):
    place[...] = (
        slots[...] == lax.broadcasted_iota(jnp.int32, place.shape, 0)
    ).astype(F32).astype(BF16)


def middle_kernel(groups, where, place, own, *refs):
    pieces, out, arrived = refs[:groups], refs[-2], refs[-1]
    me = where[0]
    for d in range(groups):
        start = pl.multiple_of((me ^ d) * CAP, CAP)
        arrived[pl.ds(start, CAP), :] = pieces[d][...]
    delta = lax.dot_general(
        place[...], arrived[...], (((0,), (0,)), ((), ())), preferred_element_type=F32
    )
    out[...] = own[...] + delta


def final_kernel(middle, other, out):
    out[...] = (middle[...] + other[...]).astype(BF16)


def few_groups(
    tokens, gate_weight, down_panels, up_panels, adapter_scales, adapter_per_row, storage_index_map
):
    groups = lax.axis_size("rows")
    me = lax.axis_index("rows").astype(jnp.int32)
    core = lax.axis_index("tp").astype(jnp.int32)
    part, depth = tokens.shape
    rows = part * groups
    rank = down_panels.shape[1]
    width = up_panels.shape[-1]
    where = me.reshape(1)
    adapter = adapter_per_row.reshape(1, rows)
    swap = [(0, 1), (1, 0)]

    def to(x, d):
        return lax.ppermute(x, "rows", [(i, i ^ d) for i in range(groups)])

    def params(limit):
        return pltpu.CompilerParams(vmem_limit_bytes=limit << 20)

    tile, buffers, ready = 256, 5, 4
    both = jnp.stack([me, core])
    slot, ahead = pl.pallas_call(
        slots_kernel,
        out_shape=[
            jax.ShapeDtypeStruct((1, rows), jnp.int32),
            jax.ShapeDtypeStruct((depth, ready * tile), BF16),
        ],
        in_specs=[SMEM, SMEM, VMEM, ANY],
        out_specs=[VMEM, VMEM],
        scratch_shapes=[pltpu.SemaphoreType.DMA((1,))],
        compiler_params=params(37),
        cost_estimate=pl.CostEstimate(flops=10**11, bytes_accessed=10**8, transcendentals=0),
        name="slots",
    )(both, storage_index_map, adapter, gate_weight)

    pieces = {0: tokens}
    steps = [1 << i for i in range(groups.bit_length() - 1)]
    for d in reversed(steps):
        pieces[d] = to(tokens, d)
    if groups > 2:
        pieces[groups - 1] = to(tokens, groups - 1)
    for d in range(1, groups):
        if d not in pieces:
            far = max(step for step in steps if step <= d)
            pieces[d] = to(pieces[far], d - far)
    pieces = [pieces[d] for d in range(groups)]

    low = pl.pallas_call(
        functools.partial(lowrank_kernel, groups),
        out_shape=jax.ShapeDtypeStruct((CAP, rank), F32),
        in_specs=[SMEM, VMEM] + [VMEM] * groups + [VMEM],
        out_specs=VMEM,
        scratch_shapes=[pltpu.VMEM((rows, depth), BF16)],
        compiler_params=params(8),
        cost_estimate=pl.CostEstimate(flops=10**8, bytes_accessed=2 * 10**6, transcendentals=0),
        name="lowrank",
    )(where, slot, *pieces, down_panels[0])
    low_other = lax.ppermute(low, "tp", swap)

    up = up_panels.reshape(rank * groups, width)

    def deltas(offsets, after):
        return pl.pallas_call(
            functools.partial(delta_kernel, groups, offsets),
            out_shape=[jax.ShapeDtypeStruct((CAP, width), BF16)] * len(offsets),
            in_specs=[SMEM, VMEM, VMEM, VMEM, VMEM, ANY],
            out_specs=[VMEM] * len(offsets),
            scratch_shapes=[pltpu.VMEM((len(offsets) * CAP, rank * groups), BF16)],
            compiler_params=params(8),
            cost_estimate=pl.CostEstimate(flops=10**6, bytes_accessed=10**6, transcendentals=0),
            name="delta",
        )(where, adapter_scales.reshape(1, 1), low, low_other, up, after)

    arrived = [None] * groups
    order = (0, 2, 1, 4, 5, 6, 7, 3)
    blocks = deltas(order, low)
    for d, x in zip(order[:6], blocks):
        arrived[d] = to(x, d) if d else x

    def once(block, after):
        return pl.pallas_call(
            relay_kernel,
            out_shape=jax.ShapeDtypeStruct(block.shape, block.dtype),
            in_specs=[VMEM, ANY],
            out_specs=VMEM,
            compiler_params=params(2),
            cost_estimate=pl.CostEstimate(flops=10**4, bytes_accessed=10**4, transcendentals=0),
            name="relay",
        )(block, after)

    seventh = once(blocks[6], arrived[2])
    arrived[7] = to(seventh, 7)
    eighth = once(blocks[7], arrived[1])
    arrived[3] = to(eighth, 3)

    half = jax.ShapeDtypeStruct((rows, width), F32)
    partner, own = pl.pallas_call(
        functools.partial(base_kernel, groups),
        in_specs=[SMEM] + [VMEM] * groups + [VMEM, ANY, ANY, ANY],
        out_specs=[VMEM, VMEM],
        scratch_shapes=[
            pltpu.VMEM((rows, depth), BF16),
            pltpu.VMEM((buffers, depth, tile), BF16),
            pltpu.SemaphoreType.DMA((buffers,)),
        ],
        out_shape=[half, half],
        compiler_params=params(37),
        cost_estimate=pl.CostEstimate(
            flops=4 * rows * depth * width, bytes_accessed=10**7, transcendentals=0
        ),
        name="base",
    )(both, *pieces, ahead, gate_weight, seventh, eighth)
    other = lax.ppermute(partner, "tp", swap)

    place = pl.pallas_call(
        place_kernel,
        out_shape=jax.ShapeDtypeStruct((groups * CAP, rows), BF16),
        in_specs=[VMEM],
        out_specs=VMEM,
        compiler_params=params(2),
        cost_estimate=pl.CostEstimate(flops=10**11, bytes_accessed=10**8, transcendentals=0),
        name="place",
    )(slot)

    middle = pl.pallas_call(
        functools.partial(middle_kernel, groups),
        out_shape=jax.ShapeDtypeStruct((rows, width), F32),
        in_specs=[SMEM, VMEM, VMEM] + [VMEM] * groups,
        out_specs=VMEM,
        scratch_shapes=[pltpu.VMEM((groups * CAP, width), BF16)],
        compiler_params=params(8),
        cost_estimate=pl.CostEstimate(flops=2 * 10**8, bytes_accessed=4 * 10**6, transcendentals=0),
        name="middle",
    )(where, place, own, *arrived)

    return pl.pallas_call(
        final_kernel,
        out_shape=jax.ShapeDtypeStruct((rows, width), BF16),
        in_specs=[VMEM, VMEM],
        out_specs=VMEM,
        compiler_params=params(8),
        cost_estimate=pl.CostEstimate(flops=10**6, bytes_accessed=10**6, transcendentals=0),
        name="combine",
    )(middle, other)


def on_device(*args):
    if lax.axis_size("rows") == 8:
        return few_groups(*args)
    return many_groups(*args)


def solution(mesh):
    placed = (
        P(("parts", "rows"), "tp"),
        P("tp", "rows"),
        P("rows", None, "tp"),
        P("rows", None, None, "tp", None),
        P("rows"),
        P("parts", None),
        P(),
    )
    return jax.shard_map(
        on_device, mesh=mesh, in_specs=placed, out_specs=P("parts", ("rows", "tp")), check_vma=False
    )
```

```python
import functools

import jax
import jax.numpy as jnp
from jax import lax
from jax.experimental import pallas as pl
from jax.experimental.pallas import tpu as pltpu
from jax.sharding import PartitionSpec as P

CAP = 32
F32 = jnp.float32
BF16 = jnp.bfloat16
VMEM = pl.BlockSpec(memory_space=pltpu.VMEM)
SMEM = pl.BlockSpec(memory_space=pltpu.SMEM)
ANY = pl.BlockSpec(memory_space=pl.ANY)


def slot_layout(adapter_per_row, storage_index_map, owner_indices, slot_depth):
    row_total = adapter_per_row.shape[0]
    stored = jnp.take(storage_index_map, adapter_per_row[:, 0], axis=0)
    row_order = jnp.argsort(stored, stable=True)
    arranged = jnp.take(stored, row_order, axis=0)
    matches = (stored[:, None] == jnp.arange(owner_indices, dtype=jnp.int32)[None, :]).astype(
        jnp.int32
    )
    counts = jnp.sum(matches, axis=0)
    starts = jnp.cumsum(counts) - counts
    within = jnp.arange(row_total, dtype=jnp.int32) - jnp.take(starts, arranged, axis=0)
    placed = arranged * slot_depth + within
    slot_of_row = jnp.zeros((row_total,), jnp.int32).at[row_order].set(placed)
    row_of_slot = (
        jnp.full((owner_indices * slot_depth,), row_total, jnp.int32)
        .at[slot_of_row]
        .set(jnp.arange(row_total, dtype=jnp.int32))
    )
    return (slot_of_row, row_of_slot)


def many_groups(
    tokens, gate_weight, down_panels, up_panels, adapter_scales, adapter_per_row, storage_index_map
):
    owner_indices = lax.axis_size("rows")
    myself = lax.axis_index("rows")
    slot_of_row, row_of_slot = slot_layout(adapter_per_row, storage_index_map, owner_indices, CAP)
    my_rows = lax.dynamic_slice_in_dim(row_of_slot, myself * CAP, CAP, 0)
    piece = lax.all_gather(tokens, "rows", axis=0, tiled=True)
    inside = my_rows < piece.shape[0]
    taken = jnp.take(piece, jnp.clip(my_rows, 0, piece.shape[0] - 1), axis=0)
    selected = jnp.where(inside[:, None], taken, jnp.zeros_like(taken))
    block = jnp.dot(piece, gate_weight, preferred_element_type=F32)
    halves = lax.psum_scatter(block, "tp", scatter_dimension=1, tiled=True)
    width = up_panels.shape[-1]
    low = lax.dot_general(
        selected, down_panels[0], (((1,), (1,)), ((), ())), preferred_element_type=F32
    )
    low = low + lax.ppermute(low, "tp", [(0, 1), (1, 0)])
    low = (low * adapter_scales[0]).astype(BF16)
    panel = up_panels.reshape(down_panels.shape[1], owner_indices, width)
    delta = jnp.einsum("cr,rof->ocf", low, panel, preferred_element_type=F32).astype(BF16)
    arrived = lax.all_to_all(delta, "rows", split_axis=0, concat_axis=0, tiled=True)
    delta_rows = jnp.take(arrived.reshape(owner_indices * CAP, width), slot_of_row, axis=0)
    return (halves + delta_rows.astype(F32)).astype(BF16)


def slots_as_row(adapter_ref, map_ref):
    rows = adapter_ref.shape[1]
    count = map_ref.shape[0]
    adapter = adapter_ref[...]
    stored = jnp.zeros_like(adapter)
    for a in range(count):
        stored = jnp.where(adapter == a, map_ref[a], stored)
    index = lax.broadcasted_iota(jnp.int32, (count, rows), 0)
    match = (stored == index).astype(F32)
    earlier = (
        lax.broadcasted_iota(jnp.int32, (rows, rows), 0)
        < lax.broadcasted_iota(jnp.int32, (rows, rows), 1)
    ).astype(F32)
    before = jnp.dot(match.astype(BF16), earlier.astype(BF16), preferred_element_type=F32)
    within = jnp.sum(match * before, axis=0, keepdims=True)
    return stored * CAP + within.astype(jnp.int32)


def slots_kernel(where, index_map, adapter, weight, slot, ahead, arrival):
    width = weight.shape[1] // 2
    start = pl.multiple_of((1 - where[1]) * width, 128)
    copy = pltpu.make_async_copy(weight.at[:, pl.ds(start, ahead.shape[1])], ahead, arrival.at[0])
    copy.start()
    slot[...] = slots_as_row(adapter, index_map)
    copy.wait()


def lowrank_kernel(groups, *refs):
    where, slots = refs[:2]
    pieces = refs[2 : 2 + groups]
    down, out, gathered = refs[2 + groups :]
    me = where[0]
    part = pieces[0].shape[0]
    for d in range(groups):
        start = pl.multiple_of((me ^ d) * part, part)
        gathered[pl.ds(start, part), :] = pieces[d][...]
    slot = slots[...]
    rows = slot.shape[1]
    mine = lax.broadcasted_iota(jnp.int32, (CAP, rows), 0) + me * CAP
    chosen = (slot == mine).astype(F32).astype(BF16)
    selected = jnp.dot(chosen, gathered[...], preferred_element_type=F32).astype(BF16)
    out[...] = lax.dot_general(
        selected, down[...], (((1,), (1,)), ((), ())), preferred_element_type=F32
    )


def relay_kernel(block, _, out):
    out[...] = block[...]


def delta_kernel(groups, offsets, where, scale, low_a, low_b, up, _, *refs):
    outs, spread = refs[:-1], refs[-1]
    me = where[0]
    rank = low_a.shape[1]
    low = ((low_a[...] + low_b[...]) * scale[...]).astype(BF16)
    depth = rank * groups
    widen = (
        lax.broadcasted_iota(jnp.int32, (rank, depth), 0)
        == lax.broadcasted_iota(jnp.int32, (rank, depth), 1) // groups
    ).astype(F32).astype(BF16)
    wide = jnp.dot(low, widen, preferred_element_type=F32)
    block = lax.rem(lax.broadcasted_iota(jnp.int32, (CAP, depth), 1), groups)
    for i, d in enumerate(offsets):
        spread[i * CAP : (i + 1) * CAP, :] = jnp.where(block == (me ^ d), wide, 0.0).astype(BF16)
    result = jnp.dot(spread[...], up[...], preferred_element_type=F32).astype(BF16)
    for i, out in enumerate(outs):
        out[...] = result[i * CAP : (i + 1) * CAP, :]


def base_kernel(groups, *refs):
    where = refs[0]
    pieces = refs[1 : 1 + groups]
    ahead, weight, _, _, partner, own, gathered, held, arrival = refs[1 + groups :]
    me, core = where[0], where[1]
    part = pieces[0].shape[0]
    width = own.shape[1]
    slots, _, tile = held.shape
    ready = ahead.shape[1] // tile
    count = width // tile
    last = 2 * count

    def fetch(step):
        half = 1 - core if step < count else core
        start = half * width + (step % count) * tile
        return pltpu.make_async_copy(
            weight.at[:, pl.ds(pl.multiple_of(start, 128), tile)],
            held.at[step % slots],
            arrival.at[step % slots],
        )

    for step in range(ready, ready + slots - 1):
        fetch(step).start()
    for d in range(groups):
        start = pl.multiple_of((me ^ d) * part, part)
        gathered[pl.ds(start, part), :] = pieces[d][...]
    for step in range(last):
        if step < ready:
            columns = ahead[:, step * tile : (step + 1) * tile]
        else:
            if step + slots - 1 < last:
                fetch(step + slots - 1).start()
            fetch(step).wait()
            columns = held[step % slots]
        out = partner if step < count else own
        start = (step % count) * tile
        out[:, start : start + tile] = jnp.dot(
            gathered[...], columns, preferred_element_type=F32
        )


def place_kernel(slots, place):
    place[...] = (
        slots[...] == lax.broadcasted_iota(jnp.int32, place.shape, 0)
    ).astype(F32).astype(BF16)


def middle_kernel(groups, where, place, own, *refs):
    pieces, out, arrived = refs[:groups], refs[-2], refs[-1]
    me = where[0]
    for d in range(groups):
        start = pl.multiple_of((me ^ d) * CAP, CAP)
        arrived[pl.ds(start, CAP), :] = pieces[d][...]
    delta = lax.dot_general(
        place[...], arrived[...], (((0,), (0,)), ((), ())), preferred_element_type=F32
    )
    out[...] = own[...] + delta


def final_kernel(middle, other, out):
    out[...] = (middle[...] + other[...]).astype(BF16)


def few_groups(
    tokens, gate_weight, down_panels, up_panels, adapter_scales, adapter_per_row, storage_index_map
):
    groups = lax.axis_size("rows")
    me = lax.axis_index("rows").astype(jnp.int32)
    core = lax.axis_index("tp").astype(jnp.int32)
    part, depth = tokens.shape
    rows = part * groups
    rank = down_panels.shape[1]
    width = up_panels.shape[-1]
    where = me.reshape(1)
    adapter = adapter_per_row.reshape(1, rows)
    swap = [(0, 1), (1, 0)]

    def to(x, d):
        return lax.ppermute(x, "rows", [(i, i ^ d) for i in range(groups)])

    def params(limit):
        return pltpu.CompilerParams(vmem_limit_bytes=limit << 20)

    tile, buffers, ready = 256, 5, 3
    both = jnp.stack([me, core])
    slot, ahead = pl.pallas_call(
        slots_kernel,
        out_shape=[
            jax.ShapeDtypeStruct((1, rows), jnp.int32),
            jax.ShapeDtypeStruct((depth, ready * tile), BF16),
        ],
        in_specs=[SMEM, SMEM, VMEM, ANY],
        out_specs=[VMEM, VMEM],
        scratch_shapes=[pltpu.SemaphoreType.DMA((1,))],
        compiler_params=params(37),
        cost_estimate=pl.CostEstimate(flops=10**11, bytes_accessed=10**8, transcendentals=0),
        name="slots",
    )(both, storage_index_map, adapter, gate_weight)

    pieces = {0: tokens}
    steps = [1 << i for i in range(groups.bit_length() - 1)]
    for d in reversed(steps):
        pieces[d] = to(tokens, d)
    if groups > 2:
        pieces[groups - 1] = to(tokens, groups - 1)
    for d in range(1, groups):
        if d not in pieces:
            far = max(step for step in steps if step <= d)
            pieces[d] = to(pieces[far], d - far)
    pieces = [pieces[d] for d in range(groups)]

    low = pl.pallas_call(
        functools.partial(lowrank_kernel, groups),
        out_shape=jax.ShapeDtypeStruct((CAP, rank), F32),
        in_specs=[SMEM, VMEM] + [VMEM] * groups + [VMEM],
        out_specs=VMEM,
        scratch_shapes=[pltpu.VMEM((rows, depth), BF16)],
        compiler_params=params(8),
        cost_estimate=pl.CostEstimate(flops=10**8, bytes_accessed=2 * 10**6, transcendentals=0),
        name="lowrank",
    )(where, slot, *pieces, down_panels[0])
    low_other = lax.ppermute(low, "tp", swap)

    up = up_panels.reshape(rank * groups, width)

    def deltas(offsets, after):
        return pl.pallas_call(
            functools.partial(delta_kernel, groups, offsets),
            out_shape=[jax.ShapeDtypeStruct((CAP, width), BF16)] * len(offsets),
            in_specs=[SMEM, VMEM, VMEM, VMEM, VMEM, ANY],
            out_specs=[VMEM] * len(offsets),
            scratch_shapes=[pltpu.VMEM((len(offsets) * CAP, rank * groups), BF16)],
            compiler_params=params(8),
            cost_estimate=pl.CostEstimate(flops=10**6, bytes_accessed=10**6, transcendentals=0),
            name="delta",
        )(where, adapter_scales.reshape(1, 1), low, low_other, up, after)

    arrived = [None] * groups
    order = (0, 2, 1, 4, 5, 6, 7, 3)
    blocks = deltas(order, low)
    for d, x in zip(order[:6], blocks):
        arrived[d] = to(x, d) if d else x

    def once(block, after):
        return pl.pallas_call(
            relay_kernel,
            out_shape=jax.ShapeDtypeStruct(block.shape, block.dtype),
            in_specs=[VMEM, ANY],
            out_specs=VMEM,
            compiler_params=params(2),
            cost_estimate=pl.CostEstimate(flops=10**4, bytes_accessed=10**4, transcendentals=0),
            name="relay",
        )(block, after)

    seventh = once(blocks[6], arrived[2])
    arrived[7] = to(seventh, 7)
    eighth = once(blocks[7], arrived[1])
    arrived[3] = to(eighth, 3)

    half = jax.ShapeDtypeStruct((rows, width), F32)
    partner, own = pl.pallas_call(
        functools.partial(base_kernel, groups),
        in_specs=[SMEM] + [VMEM] * groups + [VMEM, ANY, ANY, ANY],
        out_specs=[VMEM, VMEM],
        scratch_shapes=[
            pltpu.VMEM((rows, depth), BF16),
            pltpu.VMEM((buffers, depth, tile), BF16),
            pltpu.SemaphoreType.DMA((buffers,)),
        ],
        out_shape=[half, half],
        compiler_params=params(37),
        cost_estimate=pl.CostEstimate(
            flops=4 * rows * depth * width, bytes_accessed=10**7, transcendentals=0
        ),
        name="base",
    )(both, *pieces, ahead, gate_weight, seventh, eighth)
    other = lax.ppermute(partner, "tp", swap)

    place = pl.pallas_call(
        place_kernel,
        out_shape=jax.ShapeDtypeStruct((groups * CAP, rows), BF16),
        in_specs=[VMEM],
        out_specs=VMEM,
        compiler_params=params(2),
        cost_estimate=pl.CostEstimate(flops=10**11, bytes_accessed=10**8, transcendentals=0),
        name="place",
    )(slot)

    middle = pl.pallas_call(
        functools.partial(middle_kernel, groups),
        out_shape=jax.ShapeDtypeStruct((rows, width), F32),
        in_specs=[SMEM, VMEM, VMEM] + [VMEM] * groups,
        out_specs=VMEM,
        scratch_shapes=[pltpu.VMEM((groups * CAP, width), BF16)],
        compiler_params=params(8),
        cost_estimate=pl.CostEstimate(flops=2 * 10**8, bytes_accessed=4 * 10**6, transcendentals=0),
        name="middle",
    )(where, place, own, *arrived)

    return pl.pallas_call(
        final_kernel,
        out_shape=jax.ShapeDtypeStruct((rows, width), BF16),
        in_specs=[VMEM, VMEM],
        out_specs=VMEM,
        compiler_params=params(8),
        cost_estimate=pl.CostEstimate(flops=10**6, bytes_accessed=10**6, transcendentals=0),
        name="combine",
    )(middle, other)


def on_device(*args):
    if lax.axis_size("rows") == 8:
        return few_groups(*args)
    return many_groups(*args)


def solution(mesh):
    placed = (
        P(("parts", "rows"), "tp"),
        P("tp", "rows"),
        P("rows", None, "tp"),
        P("rows", None, None, "tp", None),
        P("rows"),
        P("parts", None),
        P(),
    )
    return jax.shard_map(
        on_device, mesh=mesh, in_specs=placed, out_specs=P("parts", ("rows", "tp")), check_vma=False
    )
```

```python
import functools

import jax
import jax.numpy as jnp
from jax import lax
from jax.experimental import pallas as pl
from jax.experimental.pallas import tpu as pltpu
from jax.sharding import PartitionSpec as P

CAP = 32
F32 = jnp.float32
BF16 = jnp.bfloat16
VMEM = pl.BlockSpec(memory_space=pltpu.VMEM)
SMEM = pl.BlockSpec(memory_space=pltpu.SMEM)
ANY = pl.BlockSpec(memory_space=pl.ANY)


def slot_layout(adapter_per_row, storage_index_map, owner_indices, slot_depth):
    row_total = adapter_per_row.shape[0]
    stored = jnp.take(storage_index_map, adapter_per_row[:, 0], axis=0)
    row_order = jnp.argsort(stored, stable=True)
    arranged = jnp.take(stored, row_order, axis=0)
    matches = (stored[:, None] == jnp.arange(owner_indices, dtype=jnp.int32)[None, :]).astype(
        jnp.int32
    )
    counts = jnp.sum(matches, axis=0)
    starts = jnp.cumsum(counts) - counts
    within = jnp.arange(row_total, dtype=jnp.int32) - jnp.take(starts, arranged, axis=0)
    placed = arranged * slot_depth + within
    slot_of_row = jnp.zeros((row_total,), jnp.int32).at[row_order].set(placed)
    row_of_slot = (
        jnp.full((owner_indices * slot_depth,), row_total, jnp.int32)
        .at[slot_of_row]
        .set(jnp.arange(row_total, dtype=jnp.int32))
    )
    return (slot_of_row, row_of_slot)


def many_groups(
    tokens, gate_weight, down_panels, up_panels, adapter_scales, adapter_per_row, storage_index_map
):
    owner_indices = lax.axis_size("rows")
    myself = lax.axis_index("rows")
    slot_of_row, row_of_slot = slot_layout(adapter_per_row, storage_index_map, owner_indices, CAP)
    my_rows = lax.dynamic_slice_in_dim(row_of_slot, myself * CAP, CAP, 0)
    piece = lax.all_gather(tokens, "rows", axis=0, tiled=True)
    inside = my_rows < piece.shape[0]
    taken = jnp.take(piece, jnp.clip(my_rows, 0, piece.shape[0] - 1), axis=0)
    selected = jnp.where(inside[:, None], taken, jnp.zeros_like(taken))
    block = jnp.dot(piece, gate_weight, preferred_element_type=F32)
    halves = lax.psum_scatter(block, "tp", scatter_dimension=1, tiled=True)
    width = up_panels.shape[-1]
    low = lax.dot_general(
        selected, down_panels[0], (((1,), (1,)), ((), ())), preferred_element_type=F32
    )
    low = low + lax.ppermute(low, "tp", [(0, 1), (1, 0)])
    low = (low * adapter_scales[0]).astype(BF16)
    panel = up_panels.reshape(down_panels.shape[1], owner_indices, width)
    delta = jnp.einsum("cr,rof->ocf", low, panel, preferred_element_type=F32).astype(BF16)
    arrived = lax.all_to_all(delta, "rows", split_axis=0, concat_axis=0, tiled=True)
    delta_rows = jnp.take(arrived.reshape(owner_indices * CAP, width), slot_of_row, axis=0)
    return (halves + delta_rows.astype(F32)).astype(BF16)


def slots_as_row(adapter_ref, map_ref):
    rows = adapter_ref.shape[1]
    count = map_ref.shape[0]
    adapter = adapter_ref[...]
    stored = jnp.zeros_like(adapter)
    for a in range(count):
        stored = jnp.where(adapter == a, map_ref[a], stored)
    index = lax.broadcasted_iota(jnp.int32, (count, rows), 0)
    match = (stored == index).astype(F32)
    earlier = (
        lax.broadcasted_iota(jnp.int32, (rows, rows), 0)
        < lax.broadcasted_iota(jnp.int32, (rows, rows), 1)
    ).astype(F32)
    before = jnp.dot(match.astype(BF16), earlier.astype(BF16), preferred_element_type=F32)
    within = jnp.sum(match * before, axis=0, keepdims=True)
    return stored * CAP + within.astype(jnp.int32)


def slots_kernel(where, index_map, adapter, weight, slot, ahead, arrival):
    width = weight.shape[1] // 2
    start = pl.multiple_of((1 - where[1]) * width, 128)
    copy = pltpu.make_async_copy(weight.at[:, pl.ds(start, ahead.shape[1])], ahead, arrival.at[0])
    copy.start()
    slot[...] = slots_as_row(adapter, index_map)
    copy.wait()


def lowrank_kernel(groups, *refs):
    where, slots = refs[:2]
    pieces = refs[2 : 2 + groups]
    down, out, gathered = refs[2 + groups :]
    me = where[0]
    part = pieces[0].shape[0]
    for d in range(groups):
        start = pl.multiple_of((me ^ d) * part, part)
        gathered[pl.ds(start, part), :] = pieces[d][...]
    slot = slots[...]
    rows = slot.shape[1]
    mine = lax.broadcasted_iota(jnp.int32, (CAP, rows), 0) + me * CAP
    chosen = (slot == mine).astype(F32).astype(BF16)
    selected = jnp.dot(chosen, gathered[...], preferred_element_type=F32).astype(BF16)
    out[...] = lax.dot_general(
        selected, down[...], (((1,), (1,)), ((), ())), preferred_element_type=F32
    )


def relay_kernel(block, _, out):
    out[...] = block[...]


def delta_kernel(groups, offsets, where, scale, low_a, low_b, up, _, *refs):
    outs, spread = refs[:-1], refs[-1]
    me = where[0]
    rank = low_a.shape[1]
    low = ((low_a[...] + low_b[...]) * scale[...]).astype(BF16)
    depth = rank * groups
    widen = (
        lax.broadcasted_iota(jnp.int32, (rank, depth), 0)
        == lax.broadcasted_iota(jnp.int32, (rank, depth), 1) // groups
    ).astype(F32).astype(BF16)
    wide = jnp.dot(low, widen, preferred_element_type=F32)
    block = lax.rem(lax.broadcasted_iota(jnp.int32, (CAP, depth), 1), groups)
    for i, d in enumerate(offsets):
        spread[i * CAP : (i + 1) * CAP, :] = jnp.where(block == (me ^ d), wide, 0.0).astype(BF16)
    result = jnp.dot(spread[...], up[...], preferred_element_type=F32).astype(BF16)
    for i, out in enumerate(outs):
        out[...] = result[i * CAP : (i + 1) * CAP, :]


def base_kernel(groups, *refs):
    where = refs[0]
    pieces = refs[1 : 1 + groups]
    ahead, weight, _, _, partner, own, gathered, held, arrival = refs[1 + groups :]
    me, core = where[0], where[1]
    part = pieces[0].shape[0]
    width = own.shape[1]
    slots, _, tile = held.shape
    ready = ahead.shape[1] // tile
    count = width // tile
    last = 2 * count

    def fetch(step):
        half = 1 - core if step < count else core
        start = half * width + (step % count) * tile
        return pltpu.make_async_copy(
            weight.at[:, pl.ds(pl.multiple_of(start, 128), tile)],
            held.at[step % slots],
            arrival.at[step % slots],
        )

    for step in range(ready, ready + slots - 1):
        fetch(step).start()
    for d in range(groups):
        start = pl.multiple_of((me ^ d) * part, part)
        gathered[pl.ds(start, part), :] = pieces[d][...]
    for step in range(last):
        if step < ready:
            columns = ahead[:, step * tile : (step + 1) * tile]
        else:
            if step + slots - 1 < last:
                fetch(step + slots - 1).start()
            fetch(step).wait()
            columns = held[step % slots]
        out = partner if step < count else own
        start = (step % count) * tile
        out[:, start : start + tile] = jnp.dot(
            gathered[...], columns, preferred_element_type=F32
        )


def place_kernel(slots, place):
    place[...] = (
        slots[...] == lax.broadcasted_iota(jnp.int32, place.shape, 0)
    ).astype(F32).astype(BF16)


def middle_kernel(groups, where, place, own, *refs):
    pieces, out, arrived = refs[:groups], refs[-2], refs[-1]
    me = where[0]
    for d in range(groups):
        start = pl.multiple_of((me ^ d) * CAP, CAP)
        arrived[pl.ds(start, CAP), :] = pieces[d][...]
    delta = lax.dot_general(
        place[...], arrived[...], (((0,), (0,)), ((), ())), preferred_element_type=F32
    )
    out[...] = own[...] + delta


def final_kernel(middle, other, out):
    out[...] = (middle[...] + other[...]).astype(BF16)


def few_groups(
    tokens, gate_weight, down_panels, up_panels, adapter_scales, adapter_per_row, storage_index_map
):
    groups = lax.axis_size("rows")
    me = lax.axis_index("rows").astype(jnp.int32)
    core = lax.axis_index("tp").astype(jnp.int32)
    part, depth = tokens.shape
    rows = part * groups
    rank = down_panels.shape[1]
    width = up_panels.shape[-1]
    where = me.reshape(1)
    adapter = adapter_per_row.reshape(1, rows)
    swap = [(0, 1), (1, 0)]

    def to(x, d):
        return lax.ppermute(x, "rows", [(i, i ^ d) for i in range(groups)])

    def params(limit):
        return pltpu.CompilerParams(vmem_limit_bytes=limit << 20)

    tile, buffers, ready = 256, 5, 3
    both = jnp.stack([me, core])
    slot, ahead = pl.pallas_call(
        slots_kernel,
        out_shape=[
            jax.ShapeDtypeStruct((1, rows), jnp.int32),
            jax.ShapeDtypeStruct((depth, ready * tile), BF16),
        ],
        in_specs=[SMEM, SMEM, VMEM, ANY],
        out_specs=[VMEM, VMEM],
        scratch_shapes=[pltpu.SemaphoreType.DMA((1,))],
        compiler_params=params(37),
        cost_estimate=pl.CostEstimate(flops=10**11, bytes_accessed=10**8, transcendentals=0),
        name="slots",
    )(both, storage_index_map, adapter, gate_weight)

    pieces = {0: tokens}
    steps = [1 << i for i in range(groups.bit_length() - 1)]
    for d in reversed(steps):
        pieces[d] = to(tokens, d)
    if groups > 2:
        pieces[groups - 1] = to(tokens, groups - 1)
    for d in range(1, groups):
        if d not in pieces:
            far = max(step for step in steps if step <= d)
            pieces[d] = to(pieces[far], d - far)
    pieces = [pieces[d] for d in range(groups)]

    low = pl.pallas_call(
        functools.partial(lowrank_kernel, groups),
        out_shape=jax.ShapeDtypeStruct((CAP, rank), F32),
        in_specs=[SMEM, VMEM] + [VMEM] * groups + [VMEM],
        out_specs=VMEM,
        scratch_shapes=[pltpu.VMEM((rows, depth), BF16)],
        compiler_params=params(8),
        cost_estimate=pl.CostEstimate(flops=10**8, bytes_accessed=2 * 10**6, transcendentals=0),
        name="lowrank",
    )(where, slot, *pieces, down_panels[0])
    low_other = lax.ppermute(low, "tp", swap)

    up = up_panels.reshape(rank * groups, width)

    def deltas(offsets, after):
        return pl.pallas_call(
            functools.partial(delta_kernel, groups, offsets),
            out_shape=[jax.ShapeDtypeStruct((CAP, width), BF16)] * len(offsets),
            in_specs=[SMEM, VMEM, VMEM, VMEM, VMEM, ANY],
            out_specs=[VMEM] * len(offsets),
            scratch_shapes=[pltpu.VMEM((len(offsets) * CAP, rank * groups), BF16)],
            compiler_params=params(8),
            cost_estimate=pl.CostEstimate(flops=10**6, bytes_accessed=10**6, transcendentals=0),
            name="delta",
        )(where, adapter_scales.reshape(1, 1), low, low_other, up, after)

    arrived = [None] * groups
    order = (0, 2, 1, 4, 5, 7, 6, 3)
    blocks = deltas(order, low)
    for d, x in zip(order[:6], blocks):
        arrived[d] = to(x, d) if d else x

    def once(block, after):
        return pl.pallas_call(
            relay_kernel,
            out_shape=jax.ShapeDtypeStruct(block.shape, block.dtype),
            in_specs=[VMEM, ANY],
            out_specs=VMEM,
            compiler_params=params(2),
            cost_estimate=pl.CostEstimate(flops=10**4, bytes_accessed=10**4, transcendentals=0),
            name="relay",
        )(block, after)

    seventh = once(blocks[6], arrived[2])
    arrived[6] = to(seventh, 6)
    eighth = once(blocks[7], arrived[1])
    arrived[3] = to(eighth, 3)

    half = jax.ShapeDtypeStruct((rows, width), F32)
    partner, own = pl.pallas_call(
        functools.partial(base_kernel, groups),
        in_specs=[SMEM] + [VMEM] * groups + [VMEM, ANY, ANY, ANY],
        out_specs=[VMEM, VMEM],
        scratch_shapes=[
            pltpu.VMEM((rows, depth), BF16),
            pltpu.VMEM((buffers, depth, tile), BF16),
            pltpu.SemaphoreType.DMA((buffers,)),
        ],
        out_shape=[half, half],
        compiler_params=params(37),
        cost_estimate=pl.CostEstimate(
            flops=4 * rows * depth * width, bytes_accessed=10**7, transcendentals=0
        ),
        name="base",
    )(both, *pieces, ahead, gate_weight, seventh, eighth)
    other = lax.ppermute(partner, "tp", swap)

    place = pl.pallas_call(
        place_kernel,
        out_shape=jax.ShapeDtypeStruct((groups * CAP, rows), BF16),
        in_specs=[VMEM],
        out_specs=VMEM,
        compiler_params=params(2),
        cost_estimate=pl.CostEstimate(flops=10**11, bytes_accessed=10**8, transcendentals=0),
        name="place",
    )(slot)

    middle = pl.pallas_call(
        functools.partial(middle_kernel, groups),
        out_shape=jax.ShapeDtypeStruct((rows, width), F32),
        in_specs=[SMEM, VMEM, VMEM] + [VMEM] * groups,
        out_specs=VMEM,
        scratch_shapes=[pltpu.VMEM((groups * CAP, width), BF16)],
        compiler_params=params(8),
        cost_estimate=pl.CostEstimate(flops=2 * 10**8, bytes_accessed=4 * 10**6, transcendentals=0),
        name="middle",
    )(where, place, own, *arrived)

    return pl.pallas_call(
        final_kernel,
        out_shape=jax.ShapeDtypeStruct((rows, width), BF16),
        in_specs=[VMEM, VMEM],
        out_specs=VMEM,
        compiler_params=params(8),
        cost_estimate=pl.CostEstimate(flops=10**6, bytes_accessed=10**6, transcendentals=0),
        name="combine",
    )(middle, other)


def on_device(*args):
    if lax.axis_size("rows") == 8:
        return few_groups(*args)
    return many_groups(*args)


def solution(mesh):
    placed = (
        P(("parts", "rows"), "tp"),
        P("tp", "rows"),
        P("rows", None, "tp"),
        P("rows", None, None, "tp", None),
        P("rows"),
        P("parts", None),
        P(),
    )
    return jax.shard_map(
        on_device, mesh=mesh, in_specs=placed, out_specs=P("parts", ("rows", "tp")), check_vma=False
    )
```
